32 devices in a mesh: layer: 2 (over y), prow: 4 (over x, core), pcol: 4 (over z).
Axes of the slice: x: 2, y: 2, z: 4, core: 2. Of those that a mesh axis runs over, the one named last changes fastest.
Arguments:
- subtree_right_hand: bfloat16 [2, 6144, 512], P('layer', ('prow', 'pcol')), may hold values from -6 to 6
- root_rhs: bfloat16 [2048, 512], P(('prow', 'pcol')), may hold values from -6 to 6
- blocks: bfloat16 [2, 6, 4, 4, 4, 4, 128, 128], P('layer', None, 'prow', 'pcol'), may hold values from -0.1875 to 0.1875
- pattern: int32 [2, 6, 4, 4, 4, 4], P('layer', None, 'prow', 'pcol'), may hold values 0 or 1
- forest_inverse: float32 [2, 3, 4, 4, 128, 128], P('layer', None, 'prow', 'pcol'), may hold values from -0.5 to 0.5
- root_inverse: float32 [4, 4, 128, 128], P('prow', 'pcol'), may hold values from -0.5 to 0.5
Outputs:
- forest_solution: bfloat16 [2, 6144, 512], P('layer', ('prow', 'pcol'))
- root_solution: bfloat16 [2048, 512], P(('prow', 'pcol'))
The draws below stay inside these ranges and needn't reach their ends.
All inputs are finite; a program needn't handle non-finite values. No bound on the sum of `pattern` on one device may be relied on, other than what follows from the above.
Results may differ from the reference program's by a relative error of at most 0.0057.
Values may be sent and summed in bfloat16 or wider, within the bound.
No kernel may reach another device: no remote copies, remote signals or barrier semaphores. Data moves between devices by JAX's collectives and lax.ppermute only.
A program may use at most 64 MiB of HBM per device.

```python
import jax
import jax.numpy as jnp
from jax import lax

SUPER = 128
RHS = 512
PAIRS = 6
GRID = 4
SUBTREE_UNKNOWNS = 6144
ROOT_ROWS = 2048
N_LAYER = 2


def place_ends(drawn, stream_key, low, largest):
    spot = [jax.random.randint(jax.random.fold_in(stream_key, axis), (), 0, length) for axis, length in enumerate(drawn.shape)]
    longest = drawn.shape.index(max(drawn.shape))
    beside = spot[:longest] + [(spot[longest] + 1) % drawn.shape[longest]] + spot[longest + 1:]
    return drawn.at[tuple(spot)].set(low).at[tuple(beside)].set(largest)


def raised(values, key, source, target, shards_of, factor):
    owner, partner = [(jnp.arange(values.shape[position]) // (values.shape[position] // shards_of)).reshape([-1 if axis == position else 1 for axis in range(values.ndim)]) for position in (source, target)]
    chosen = jax.random.permutation(key, shards_of)[partner]
    strong = (owner == chosen) | (owner == (partner + shards_of // 2) % shards_of)
    return jnp.where(strong, factor * values, values)


def block_levels(stream_key, dims, pieces, low, high):
    def one(dim, parts):
        steps = jax.random.uniform(jax.random.fold_in(jax.random.fold_in(stream_key, 6), dim), (parts,), jnp.float32, low / len(pieces), high / len(pieces))
        return jnp.repeat(jnp.exp(steps), dims[dim] // parts).reshape((-1,) + (1,) * (len(dims) - dim - 1))

    factor_of = one(*pieces[0])
    for cut in pieces[1:]:
        factor_of = factor_of * one(*cut)
    return factor_of


def normal_values(stream_key, dims, width, most, shards=(), held_as=jnp.bfloat16):
    level = block_levels(stream_key, dims, shards, -0.22, 0.18) if shards else 1.0
    values = jax.random.normal(stream_key, dims, jnp.float32) * width * level
    return jnp.minimum(jnp.maximum(values, -most), most).astype(held_as)


def heavy_noise(own_key, extent, spread, most, cuts, heavy, held_as=jnp.bfloat16):
    values = spread * jax.random.normal(own_key, extent, jnp.float32)
    if cuts:
        values = values * block_levels(own_key, extent, cuts, -0.22, 0.18)
    return jnp.clip(raised(values, jax.random.fold_in(own_key, 3), *heavy), -most, most).astype(held_as)


def setup_inputs(seed: int = 0) -> dict:
    key_list = jax.random.split(jax.random.key(seed), 7)
    subtree_right_hand = normal_values(key_list[0], (N_LAYER, SUBTREE_UNKNOWNS, RHS), 1.0, 6.0, ((0, 2), (1, 16)))
    root_rhs = normal_values(key_list[1], (ROOT_ROWS, RHS), 1.0, 6.0, ((0, 16),))
    blocks = heavy_noise(key_list[2], (N_LAYER, PAIRS, GRID, GRID, GRID, GRID, SUPER, SUPER), (GRID * GRID * SUPER) ** -0.5, 0.1875, ((0, 2), (2, 4), (3, 4)), (3, 4, 4, 2.0))
    pattern = place_ends((jax.random.randint(key_list[3], (N_LAYER, PAIRS, GRID, GRID, GRID, GRID), 0, 2) < 1).astype(jnp.int32), jax.random.fold_in(key_list[3], 1), 0, 1)
    forest_inverse = normal_values(key_list[4], (N_LAYER, 3, GRID, GRID, SUPER, SUPER), SUPER ** -0.5, 0.5, ((0, 2), (2, 4), (3, 4)), jnp.float32)
    root_inverse = normal_values(key_list[5], (GRID, GRID, SUPER, SUPER), SUPER ** -0.5, 0.5, ((0, 4), (1, 4)), jnp.float32)
    return {"subtree_right_hand": subtree_right_hand, "root_rhs": root_rhs, "blocks": blocks, "pattern": pattern, "forest_inverse": forest_inverse, "root_inverse": root_inverse}


def pair_slot(source, target):
    return (0, 3, 5)[source] + target - source - 1


def to_supernodes(flat_rows, levels):
    shaped = flat_rows.reshape(GRID, GRID, levels, GRID, SUPER // GRID, RHS)
    return shaped.transpose(2, 3, 0, 1, 4, 5).reshape(levels, GRID, GRID, SUPER, RHS)


def flatten_blocks(supernodes, levels):
    shaped = supernodes.reshape(levels, GRID, GRID, GRID, SUPER // GRID, RHS)
    return shaped.transpose(2, 3, 0, 1, 4, 5).reshape(GRID * GRID * levels * SUPER, RHS)


def contribution(block_entries, block_mask, solution):
    factor_weights = block_entries.astype(jnp.float32) * block_mask.astype(jnp.float32)[..., None, None]
    return jnp.einsum("acbdxy,dcyr->abxr", factor_weights, solution.astype(jnp.float32), precision=lax.Precision.HIGHEST)


def solve_blocks(inverse, right_hand_side):
    product = jnp.einsum("abxy,abyr->abxr", inverse, right_hand_side, precision=lax.Precision.HIGHEST)
    return product.astype(jnp.bfloat16)


def reference(subtree_right_hand, root_rhs, blocks, pattern, forest_inverse, root_inverse):
    forest_out = []
    root_terms = jnp.zeros((GRID, GRID, SUPER, RHS), jnp.float32)
    for layer_index in range(N_LAYER):
        right_blocks = to_supernodes(subtree_right_hand[layer_index], 3)
        solved = []
        for target in range(3):
            incoming = jnp.zeros((GRID, GRID, SUPER, RHS), jnp.float32)
            for source in range(target):
                slot = pair_slot(source, target)
                incoming = incoming + contribution(blocks[layer_index, slot], pattern[layer_index, slot], solved[source])
            right_hand_side = right_blocks[target].astype(jnp.float32) - incoming
            solved.append(solve_blocks(forest_inverse[layer_index, target], right_hand_side))
        layer_terms = jnp.zeros((GRID, GRID, SUPER, RHS), jnp.float32)
        for source in range(3):
            slot = pair_slot(source, 3)
            layer_terms = layer_terms + contribution(blocks[layer_index, slot], pattern[layer_index, slot], solved[source])
        root_terms = root_terms + layer_terms
        forest_out.append(flatten_blocks(jnp.stack(solved), 3))
    root_blocks = to_supernodes(root_rhs, 1)
    root_solved = solve_blocks(root_inverse, root_blocks[0].astype(jnp.float32) - root_terms)
    return jnp.stack(forest_out), flatten_blocks(root_solved[None], 1)
```

```python
import functools

import jax
import jax.numpy as jnp
from jax import lax
from jax.experimental import pallas as pl
from jax.experimental.pallas import tpu as pltpu
from jax.sharding import PartitionSpec as P

F32 = jnp.float32
BF16 = jnp.bfloat16
VMEM = pltpu.VMEM
PARAMS = pltpu.CompilerParams(vmem_limit_bytes=32 * 1024 * 1024)
PAIR = {(0, 1): 0, (0, 2): 1, (0, 3): 2, (1, 2): 3, (1, 3): 4, (2, 3): 5}


def whole(count):
    return [pl.BlockSpec(memory_space=VMEM)] * count


def call(kernel, outs, *args, scratch=(), in_specs=None, grid=None):
    extra = {}
    if grid is not None:
        extra["grid"] = grid
    return pl.pallas_call(
        kernel,
        out_shape=[jax.ShapeDtypeStruct(shape, dtype) for shape, dtype in outs],
        in_specs=whole(len(args)) if in_specs is None else in_specs,
        out_specs=whole(len(outs)),
        scratch_shapes=list(scratch),
        compiler_params=PARAMS,
        **extra,
    )(*args)


def dot(left, right):
    return jnp.dot(left, right, preferred_element_type=F32)


def split(value):
    high = value.astype(BF16)
    return high, (value - high.astype(F32)).astype(BF16)


def precise(inverse, value):
    ih, il = split(inverse)
    vh, vl = split(value)
    return dot(
        jnp.concatenate([ih, ih, il], axis=1), jnp.concatenate([vh, vl, vh], axis=0)
    )


def pack_kernel(forest, root, inverse, own, *sends):
    a = lax.axis_index("prow")
    high, low = split(inverse[...])
    half = high.shape[0] // 2
    packed = jnp.concatenate([high[:half], high[half:], low[:half], low[half:]], axis=1)
    own[...] = packed
    for k in range(1, 4):
        first, later = sends[k - 1], sends[k + 2]
        first[:half] = packed
        first[half:] = forest[1, a ^ k]
        later[0] = forest[2, a ^ k]
        later[1] = root[a ^ k]


def mask_kernel(pattern, blocks, out):
    a, b = lax.axis_index("prow"), lax.axis_index("pcol")
    n = pl.program_id(0)
    size = blocks.shape[-1]
    for j in range(4):
        for k in range(4):
            keep = pattern[n, b ^ j, a ^ k]
            block = blocks[0, b ^ j, a ^ k]
            out[0, j, :, k * size : (k + 1) * size] = jnp.where(
                keep != 0, block, jnp.zeros_like(block)
            )


def inject(acc, own, others, slot):
    a, b = lax.axis_index("prow"), lax.axis_index("pcol")
    rows = own.shape[-2]
    acc[...] = jnp.zeros_like(acc)
    place = pl.ds(pl.multiple_of(b * rows, rows), rows)
    for k in range(4):
        value = (own[slot[0], a] if k == 0 else others[k - 1][slot[1]]).astype(F32)
        acc[a ^ b ^ k, place, :] = value


def first_kernel(g0, g1, g2, g3, packed, m1, m2, m3, forest, weights, *rest):
    solved, turned, o0, o1, o2, o3, rows, acc = rest
    a = lax.axis_index("prow")
    part = g0.shape[-2]
    size = 4 * part
    half = size // 2
    for j, piece in enumerate((g0, g1, g2, g3)):
        place = pl.ds(pl.multiple_of((a ^ j) * part, part), part)
        for u in range(4):
            rows[u, place, :] = piece[u]
    for j, message in enumerate((packed, m1, m2, m3)):
        value = message[:half]
        high = jnp.concatenate([value[:, :size], value[:, size : 2 * size]], axis=0)
        low = jnp.concatenate(
            [value[:, 2 * size : 3 * size], value[:, 3 * size :]], axis=0
        )
        side = rows[a ^ j]
        answer = dot(
            jnp.concatenate([high, low], axis=1), jnp.concatenate([side, side], axis=0)
        )
        solved[j * size : (j + 1) * size] = answer.astype(BF16)
    for j in range(4):
        turned[a ^ j] = solved[pl.ds(pl.multiple_of(j * size + a * part, part), part)]
    b = lax.axis_index("pcol")
    acc[...] = jnp.zeros_like(acc)
    place = pl.ds(pl.multiple_of(b * part, part), part)
    for k, message in enumerate((None, m1, m2, m3)):
        value = forest[1, a] if k == 0 else message[half:]
        acc[a ^ b ^ k, place, :] = value.astype(F32)
    for j, out in enumerate((o0, o1, o2, o3)):
        out[...] = (acc[j] - dot(weights[0, j], solved[...])).astype(out.dtype)


def solve_kernel(own, r1, r2, r3, inverse, out):
    value = own[...] + r1[...].astype(F32) + r2[...].astype(F32) + r3[...].astype(F32)
    out[...] = precise(inverse[...], value).astype(out.dtype)


def middle_kernel(s0, s1, s2, s3, weights, acc, *rest):
    solved, turned, o0, o1, o2, o3 = rest
    a = lax.axis_index("prow")
    size = s0.shape[0]
    part = size // 4
    for j, piece in enumerate((s0, s1, s2, s3)):
        solved[j * size : (j + 1) * size] = piece[...]
        turned[a ^ j] = piece[pl.ds(pl.multiple_of(a * part, part), part)]
    for j, out in enumerate((o0, o1, o2, o3)):
        out[...] = (acc[j] - dot(weights[0, j], solved[...])).astype(out.dtype)


def early_kernel(solved, w2, w3, forest, root, c1, c2, c3, acc2, acc3):
    layer = lax.axis_index("layer")
    inject(acc2, forest, (c1, c2, c3), (2, 0))
    inject(acc3, root, (c1, c2, c3), (0, 1))
    first = (layer == 0).astype(F32)
    for j in range(4):
        acc2[j] -= dot(w2[0, j], solved[...])
        acc3[j] = acc3[j] * first - dot(w3[0, j], solved[...])


def later_kernel(solved, weights, acc, out):
    for j in range(4):
        out[j] = acc[j] - dot(weights[0, j], solved[...])


def root_kernel(s0, s1, s2, s3, weights, acc, i0, i1, i2, i3, *rest):
    turned, o0, o1, o2, o3, solved, full = rest
    a, b = lax.axis_index("prow"), lax.axis_index("pcol")
    size = s0.shape[0]
    part = size // 4
    for j, piece in enumerate((s0, s1, s2, s3)):
        solved[j * size : (j + 1) * size] = piece[...]
        turned[a ^ j] = piece[pl.ds(pl.multiple_of(a * part, part), part)]
    for j, inverse in enumerate((i0, i1, i2, i3)):
        full[b ^ j] = precise(inverse[...], acc[j] - dot(weights[0, j], solved[...]))
    for j, out in enumerate((o0, o1, o2, o3)):
        place = pl.ds(pl.multiple_of((b ^ j) * part, part), part)
        out[...] = full[:, place, :].astype(out.dtype)


def total_kernel(own, r1, r2, r3, out):
    value = own[...] + r1[...].astype(F32) + r2[...].astype(F32) + r3[...].astype(F32)
    for layer in range(out.shape[0]):
        out[layer] = value.astype(out.dtype)


def join_kernel(pieces, out):
    out[...] = (pieces[0].astype(F32) + pieces[1].astype(F32)).astype(out.dtype)


def shards(subtree_right_hand, root_rhs, blocks, pattern, forest_inverse, root_inverse):
    layers = lax.axis_size("layer")
    size = blocks.shape[-1]
    part = size // 4
    cols = subtree_right_hand.shape[-1]
    forest = subtree_right_hand.reshape(3, 4, part, cols)
    root = root_rhs.reshape(4, part, cols)
    blocks = blocks.reshape(6, 4, 4, size, size)
    pattern = pattern.reshape(6, 4, 4)
    inverses = forest_inverse.reshape(3, size, size)
    last_inverse = root_inverse.reshape(size, size)
    both = ("prow", "pcol")
    turn = [(i * 4 + j, j * 4 + i) for i in range(4) for j in range(4)]

    def swap(value, axis, k):
        return lax.ppermute(value, axis, [(i, i ^ k) for i in range(4)])

    def gather(value):
        far = swap(value, "prow", 2)
        return value, swap(value, "prow", 1), far, swap(far, "prow", 1)

    def spread(outs):
        return [swap(out, "pcol", k) for k, out in enumerate(outs[1:], 1)]

    def table(pair):
        return pl.BlockSpec((1, 4, size, 4 * size), lambda i: (pair, 0, 0, 0))

    def with_table(kernel, outs, at, pair, *args, scratch=()):
        specs = whole(len(args))
        for index, which in zip(at, pair):
            specs[index] = table(PAIR[which])
        return call(kernel, outs, *args, scratch=scratch, in_specs=specs, grid=(1,))

    piece = ((4, part, cols), BF16)
    partial = [((size, cols), F32)] + [((size, cols), BF16)] * 3
    sums = ((4, size, cols), F32)
    tall = ((4 * size, cols), BF16)

    side = lax.ppermute(forest[0], both, turn)
    packed, *sends = call(
        pack_kernel,
        [((size // 2, cols), BF16)]
        + [((size // 2 + part, cols), BF16)] * 3
        + [((2, part, cols), BF16)] * 3,
        forest,
        root,
        inverses[0],
    )
    early = [swap(send, "prow", k) for k, send in enumerate(sends[:3], 1)]
    weights = pl.pallas_call(
        mask_kernel,
        out_shape=jax.ShapeDtypeStruct((6, 4, size, 4 * size), BF16),
        grid=(6,),
        in_specs=[
            pl.BlockSpec(memory_space=pltpu.SMEM),
            pl.BlockSpec((1, 4, 4, size, size), lambda n: (n, 0, 0, 0, 0)),
        ],
        out_specs=pl.BlockSpec((1, 4, size, 4 * size), lambda n: (n, 0, 0, 0)),
        compiler_params=PARAMS,
    )(pattern, blocks)
    root_inverses = [last_inverse] + [swap(last_inverse, "pcol", k) for k in (1, 2, 3)]

    solved0, turned0, *outs = with_table(
        first_kernel,
        [tall, piece] + partial,
        (9,),
        ((0, 1),),
        *gather(side),
        packed,
        *early,
        forest,
        weights,
        scratch=[VMEM((4, size, cols), BF16), VMEM((4, size, cols), F32)],
    )
    got = spread(outs)
    late = [swap(send, "prow", k) for k, send in enumerate(sends[3:], 1)]
    acc2, acc3 = with_table(
        early_kernel,
        [sums, sums],
        (1, 2),
        ((0, 2), (0, 3)),
        solved0,
        weights,
        weights,
        forest,
        root[None],
        *late,
    )
    (answer,) = call(
        solve_kernel, [((size, cols), BF16)], outs[0], *got, inverses[1]
    )
    given0 = lax.ppermute(turned0, both, turn)
    solved1, turned1, *outs = with_table(
        middle_kernel,
        [tall, piece] + partial,
        (4,),
        ((1, 2),),
        *gather(answer),
        weights,
        acc2,
    )
    got = spread(outs)
    (acc3,) = with_table(later_kernel, [sums], (1,), ((1, 3),), solved1, weights, acc3)
    (answer,) = call(
        solve_kernel, [((size, cols), BF16)], outs[0], *got, inverses[2]
    )
    given1 = lax.ppermute(turned1, both, turn)
    turned2, *outs = with_table(
        root_kernel,
        [piece, ((4, part, cols), F32)] + [piece] * 3,
        (4,),
        ((2, 3),),
        *gather(answer),
        weights,
        acc3,
        *root_inverses,
        scratch=[VMEM((4 * size, cols), BF16), VMEM((4, size, cols), F32)],
    )
    got = spread(outs)
    given2 = lax.ppermute(turned2, both, turn)
    if layers == 2:
        (mine,) = call(
            total_kernel, [((2, 4, part, cols), BF16)], outs[0], *got
        )
        pieces = lax.all_to_all(
            mine.reshape(8, part, cols), ("layer", "prow"), 0, 0, tiled=True
        )
        (root_out,) = call(
            join_kernel, [((4, part, cols), BF16)], pieces.reshape(2, 4, part, cols)
        )
    else:
        (mine,) = call(total_kernel, [((1, 4, part, cols), F32)], outs[0], *got)
        mine = lax.psum(mine[0], "layer")
        root_out = lax.all_to_all(mine, "prow", 0, 0, tiled=True).astype(BF16)
    forest_out = jnp.stack([given0, given1, given2])
    return forest_out.reshape(1, 3 * size, cols), root_out.reshape(size, cols)


def solution(mesh):
    placed = (
        P("layer", ("prow", "pcol"), None),
        P(("prow", "pcol"), None),
        P("layer", None, "prow", "pcol", None, None, None, None),
        P("layer", None, "prow", "pcol", None, None),
        P("layer", None, "prow", "pcol", None, None),
        P("prow", "pcol", None, None),
    )
    return jax.shard_map(
        shards,
        mesh=mesh,
        in_specs=placed,
        out_specs=(P("layer", ("prow", "pcol"), None), P(("prow", "pcol"), None)),
        check_vma=False,
    )
```

```python
import functools

import jax
import jax.numpy as jnp
from jax import lax
from jax.experimental import pallas as pl
from jax.experimental.pallas import tpu as pltpu
from jax.sharding import PartitionSpec as P

F32 = jnp.float32
BF16 = jnp.bfloat16
VMEM = pltpu.VMEM
MIB = 1024 * 1024
PAIR = {(0, 1): 0, (0, 2): 1, (0, 3): 2, (1, 2): 3, (1, 3): 4, (2, 3): 5}


def whole(count):
    return [pl.BlockSpec(memory_space=VMEM)] * count


def call(kernel, outs, *args, scratch=(), in_specs=None, grid=None, limit=32):
    extra = {}
    if grid is not None:
        extra["grid"] = grid
    return pl.pallas_call(
        kernel,
        out_shape=[jax.ShapeDtypeStruct(shape, dtype) for shape, dtype in outs],
        in_specs=whole(len(args)) if in_specs is None else in_specs,
        out_specs=whole(len(outs)),
        scratch_shapes=list(scratch),
        compiler_params=pltpu.CompilerParams(vmem_limit_bytes=limit * MIB),
        **extra,
    )(*args)


def dot(left, right):
    return jnp.dot(left, right, preferred_element_type=F32)


def split(value):
    high = value.astype(BF16)
    return high, (value - high.astype(F32)).astype(BF16)


def precise(inverse, value):
    ih, il = split(inverse)
    vh, vl = split(value)
    return dot(
        jnp.concatenate([ih, ih, il], axis=1), jnp.concatenate([vh, vl, vh], axis=0)
    )


def crossed(index):
    return 2 * (index % 2) + index // 2


def pack_kernel(forest, root, first, last, side, *rest):
    own, near, far, *late, halved = rest[:8]
    held, top, inverse, final, sems = rest[8:]
    a = lax.axis_index("prow")
    half = inverse.shape[0] // 2
    chunks, cols = side.shape[0], side.shape[-1]
    moves = [
        pltpu.make_async_copy(forest, held, sems.at[0]),
        pltpu.make_async_copy(root, top, sems.at[1]),
        pltpu.make_async_copy(first.at[0], inverse, sems.at[2]),
        pltpu.make_async_copy(
            last.at[pl.ds(lax.axis_index("layer") % 2 * half, half)], final, sems.at[3]
        ),
    ]
    for move in moves:
        move.start()
    moves[0].wait()
    for h in range(chunks):
        side[h] = held[0, :, :, h * cols : (h + 1) * cols]
    moves[2].wait()
    high, low = split(inverse[...])
    packed = jnp.concatenate([high[:half], high[half:], low[:half], low[half:]], axis=1)
    part = held.shape[2]
    for out, slots in ((own, (0,)), (near, (1,)), (far, (2, 3))):
        out[:half] = packed
        for i, k in enumerate(slots):
            out[half + i * part : half + (i + 1) * part] = held[1, a ^ k]
    moves[1].wait()
    for k, out in enumerate(late):
        out[0] = held[2, a ^ k]
        out[1] = top[a ^ k]
    moves[3].wait()
    high, low = split(final[...])
    quarter = half // 2
    halved[...] = jnp.concatenate(
        [high[:quarter], high[quarter:], low[:quarter], low[quarter:]], axis=1
    )


def masked_pair(n, pattern, blocks, out):
    a, b = lax.axis_index("prow"), lax.axis_index("pcol")
    size = blocks.shape[-1]
    for j in range(4):
        for k in range(4):
            block = blocks[b ^ j, a ^ k]
            out[j, :, k * size : (k + 1) * size] = jnp.where(
                pattern[n, b ^ j, a ^ k] != 0, block, jnp.zeros_like(block)
            )


def mask_kernel(pattern, blocks, out, held, sems):
    pairs = out.shape[0]
    moves = [
        pltpu.make_async_copy(blocks.at[n], held.at[n], sems.at[n])
        for n in range(pairs)
    ]
    for move in moves:
        move.start()
    for n, move in enumerate(moves):
        move.wait()
        masked_pair(n, pattern, held.at[n], out.at[n])


def send_sums(acc, weights, solved, outs):
    for j, out in enumerate(outs):
        value = acc(j) - dot(weights[0, j], solved[...])
        out[: value.shape[0]] = value.astype(out.dtype)


def first_kernel(h, g0, g1, g2, g3, m0, m1, m2, m3, halved, weights, *rest):
    solved, *outs, rows, acc = rest
    a, b = lax.axis_index("prow"), lax.axis_index("pcol")
    part, cols = g0.shape[-2:]
    size = 4 * part
    half = size // 2
    for j, piece in enumerate((g0, g1, g2, g3)):
        place = pl.ds(pl.multiple_of((a ^ j) * part, part), part)
        for u in range(4):
            rows[u, place, :] = piece[u]
    acc[...] = jnp.zeros_like(acc)
    place = pl.ds(pl.multiple_of(b * part, part), part)
    for j, message in enumerate((m0, m1, m2, m3)):
        value = message[:half]
        high = jnp.concatenate([value[:, :size], value[:, size : 2 * size]], axis=0)
        low = jnp.concatenate(
            [value[:, 2 * size : 3 * size], value[:, 3 * size : 4 * size]], axis=0
        )
        right = rows[a ^ j]
        answer = dot(
            jnp.concatenate([high, low], axis=1),
            jnp.concatenate([right, right], axis=0),
        )
        solved[j * size : (j + 1) * size] = answer.astype(BF16)
        value = message[message.shape[0] - part :, h * cols : (h + 1) * cols]
        if j == 2:
            value = message[half : half + part, h * cols : (h + 1) * cols]
        acc[a ^ b ^ j, place, :] = value.astype(F32)
    send_sums(lambda j: acc[j], weights, solved, outs)
    if h == 0:
        for out in outs[1:]:
            out[size:] = halved[...]


def solve_kernel(own, r1, r2, r3, inverse, out):
    value = own[...]
    for other in (r1, r2, r3):
        value += other[: value.shape[0]].astype(F32)
    out[...] = precise(inverse[...], value).astype(out.dtype)


def middle_kernel(h, s0, s1, s2, s3, weights, acc, solved, *outs):
    size, cols = s0.shape
    for j, piece in enumerate((s0, s1, s2, s3)):
        solved[j * size : (j + 1) * size] = piece[...]
    here = slice(h * cols, (h + 1) * cols)
    send_sums(lambda j: acc[j, :, here], weights, solved, outs)


def turn_rows(solved, here, turned):
    a = lax.axis_index("prow")
    part = turned.shape[1]
    for j in range(4):
        start = 4 * part * j + crossed(a) * part
        place = pl.ds(pl.multiple_of(start, part), part)
        turned[a ^ j, :, here] = solved[place]


def early_kernel(chunks, *refs):
    solved, (w2, w3, c0, c1, c2, c3) = refs[:chunks], refs[chunks : chunks + 6]
    acc2, acc3, turned = refs[chunks + 6 :]
    a, b = lax.axis_index("prow"), lax.axis_index("pcol")
    part = c0.shape[1]
    cols = solved[0].shape[1]
    place = pl.ds(pl.multiple_of(b * part, part), part)
    top = (lax.axis_index("layer") == 0).astype(F32)
    acc2[...] = jnp.zeros_like(acc2)
    acc3[...] = jnp.zeros_like(acc3)
    for k, piece in enumerate((c0, c1, c2, c3)):
        acc2[a ^ b ^ k, place, :] = piece[0].astype(F32)
        acc3[a ^ b ^ k, place, :] = piece[1].astype(F32) * top
    for h in range(chunks):
        here = slice(h * cols, (h + 1) * cols)
        turn_rows(solved[h], here, turned)
        for j in range(4):
            acc2[j, :, here] -= dot(w2[0, j], solved[h][...])
            acc3[j, :, here] -= dot(w3[0, j], solved[h][...])


def later_kernel(chunks, *refs):
    solved, (weights, acc, out, turned) = refs[:chunks], refs[chunks:]
    cols = solved[0].shape[1]
    for h in range(chunks):
        here = slice(h * cols, (h + 1) * cols)
        turn_rows(solved[h], here, turned)
        for j in range(4):
            out[j, :, here] = acc[j, :, here] - dot(weights[0, j], solved[h][...])


def root_kernel(h, s0, s1, s2, s3, weights, acc, mine, theirs, *rest):
    turned, *outs, solved, full = rest
    b = lax.axis_index("pcol")
    size, cols = s0.shape
    part = size // 4
    for j, piece in enumerate((s0, s1, s2, s3)):
        solved[j * size : (j + 1) * size] = piece[...]
    turn_rows(solved, slice(None), turned)
    here = slice(h * cols, (h + 1) * cols)
    upper = lax.axis_index("layer") % 2 == 0
    for j in range(4):
        one, two = mine[j], theirs[j]
        inverse = jnp.concatenate(
            [jnp.where(upper, one, two), jnp.where(upper, two, one)], axis=0
        )
        value = acc[j, :, here] - dot(weights[0, j], solved[...])
        full[b ^ j] = precise(inverse, value)
    for j, out in enumerate(outs):
        place = pl.ds(pl.multiple_of((b ^ j) * part, part), part)
        out[...] = full[:, place, :].astype(out.dtype)


def halves_kernel(own, r1, r2, r3, out):
    quarter = own.shape[0]
    size = out.shape[-1]
    for j, ref in enumerate((own, r1, r2, r3)):
        value = ref[ref.shape[0] - quarter :].astype(F32)
        for i in range(2):
            high = value[:, i * size : (i + 1) * size]
            low = value[:, (2 + i) * size : (3 + i) * size]
            out[j, i * quarter : (i + 1) * quarter] = high + low


def turned_kernel(first, second, *rest):
    *third, out = rest
    out[0] = first[...]
    out[1] = second[...]
    cols = third[0].shape[-1]
    for h, piece in enumerate(third):
        out[2, :, :, h * cols : (h + 1) * cols] = piece[...]


def total_kernel(chunks, *refs):
    parts, out = refs[:-1], refs[-1]
    cols = parts[0].shape[-1]
    for h in range(chunks):
        own, *others = parts[4 * h : 4 * h + 4]
        value = own[...]
        for other in others:
            value += other[...].astype(F32)
        for layer in range(out.shape[0]):
            out[layer, :, :, h * cols : (h + 1) * cols] = value.astype(out.dtype)


def join_kernel(pieces, out):
    out[...] = (pieces[0].astype(F32) + pieces[1].astype(F32)).astype(out.dtype)


CHUNKS = 1
LARGE = 60


def shards(subtree_right_hand, root_rhs, blocks, pattern, forest_inverse, root_inverse):
    layers = lax.axis_size("layer")
    size = blocks.shape[-1]
    part, half = size // 4, size // 2
    width = subtree_right_hand.shape[-1]
    cols = width // CHUNKS
    forest = subtree_right_hand.reshape(3, 4, part, width)
    root = root_rhs.reshape(4, part, width)
    blocks = blocks.reshape(6, 4, 4, size, size)
    pattern = pattern.reshape(6, 4, 4)
    inverses = forest_inverse.reshape(3, size, size)
    last_inverse = root_inverse.reshape(size, size)
    both = ("prow", "pcol")
    turn = [(i * 4 + j, j * 4 + i) for i in range(4) for j in range(4)]
    back = [(crossed(i) * 4 + j, j * 4 + i) for i in range(4) for j in range(4)]
    hbm = pl.BlockSpec(memory_space=pltpu.HBM)
    dma = pltpu.SemaphoreType.DMA

    def after(*values):
        return lax.optimization_barrier(values)

    def swap(value, axis, k):
        return lax.ppermute(value, axis, [(i, i ^ k) for i in range(4)])

    def gather(value):
        far = swap(value, "prow", 2)
        return value, swap(value, "prow", 1), far, swap(far, "prow", 1)

    def spread(outs):
        return [swap(out, "pcol", k) for k, out in enumerate(outs[1:], 1)]

    def with_table(kernel, outs, at, pair, *args, scratch=()):
        specs = whole(len(args))
        for index, which in zip(at, pair):
            place = PAIR[which]
            specs[index] = pl.BlockSpec(
                (1, 4, size, 4 * size), lambda i, place=place: (place, 0, 0, 0)
            )
        return call(kernel, outs, *args, scratch=scratch, in_specs=specs, grid=(1,))

    piece = ((4, part, width), BF16)
    partial = [((size, cols), F32)] + [((size, cols), BF16)] * 3
    sums = ((4, size, width), F32)
    tall = ((4 * size, cols), BF16)
    every = range(CHUNKS)
    run = functools.partial

    side, *sends = call(
        pack_kernel,
        [((CHUNKS, 4, part, cols), BF16)]
        + [((half + i * part, width), BF16) for i in (1, 1, 2)]
        + [((2, part, width), BF16)] * 4
        + [((half // 2, width), BF16)],
        forest,
        root,
        inverses,
        last_inverse,
        in_specs=[hbm] * 4,
        limit=LARGE,
        scratch=[
            VMEM((3, 4, part, width), BF16),
            VMEM((4, part, width), BF16),
            VMEM((size, size), F32),
            VMEM((half, size), F32),
            dma((4,)),
        ],
    )
    side = lax.ppermute(side, both, turn)
    far = swap(sends[2], "prow", 2)
    (weights,) = call(
        mask_kernel,
        [((6, 4, size, 4 * size), BF16)],
        pattern,
        blocks,
        in_specs=[pl.BlockSpec(memory_space=pltpu.SMEM), hbm],
        scratch=[VMEM(blocks.shape, BF16), dma((6,))],
    )
    side, far, weights = after(side, far, weights)
    early = [sends[0], swap(sends[1], "prow", 1), far, swap(far, "prow", 1)]

    sides = [gather(side[h]) for h in every]
    longer = [partial[0]] + [((size + half // 2, cols), BF16)] * 3
    solved0, outs, got = {}, {}, {}
    for h in every:
        solved0[h], *outs[h] = with_table(
            run(first_kernel, h),
            [tall] + (longer if h == 0 else partial),
            (9,),
            ((0, 1),),
            *sides[h],
            *early,
            sends[7],
            weights,
            scratch=[VMEM((4, size, cols), BF16), VMEM((4, size, cols), F32)],
        )
        got[h] = spread(outs[h])
    late = after(*sends[4:7], got[0][0])[:3]
    late = [sends[3]] + [swap(late[k - 1], "prow", k) for k in (1, 2, 3)]
    *got[0], late[1], late[2], late[3] = after(*got[0], *late[1:])
    acc2, acc3, turned0 = with_table(
        run(early_kernel, CHUNKS),
        [sums, sums, piece],
        (CHUNKS, CHUNKS + 1),
        ((0, 2), (0, 3)),
        *solved0.values(),
        weights,
        weights,
        *late,
    )
    answers = {}
    for h in every:
        (answers[h],) = call(
            solve_kernel, [((size, cols), BF16)], outs[h][0], *got[h], inverses[1]
        )
    (mine,) = call(halves_kernel, [((4, half, size), F32)], sends[7], *got[0])
    solved1 = {}
    for h in every:
        solved1[h], *outs[h] = with_table(
            run(middle_kernel, h),
            [tall] + partial,
            (4,),
            ((1, 2),),
            *gather(answers[h]),
            weights,
            acc2,
        )
        got[h] = spread(outs[h])
    stacked = after(mine, got[0][0])[0]
    pairs = [(i, i ^ 1) for i in range(layers)]
    theirs = lax.ppermute(stacked, "layer", pairs)
    *got[0], theirs = after(*got[0], theirs)
    acc3, turned1 = with_table(
        run(later_kernel, CHUNKS),
        [sums, piece],
        (CHUNKS,),
        ((1, 3),),
        *solved1.values(),
        weights,
        acc3,
    )
    for h in every:
        (answers[h],) = call(
            solve_kernel, [((size, cols), BF16)], outs[h][0], *got[h], inverses[2]
        )
    turned2 = {}
    for h in every:
        turned2[h], *outs[h] = with_table(
            run(root_kernel, h),
            [((4, part, cols), BF16), ((4, part, cols), F32)]
            + [((4, part, cols), BF16)] * 3,
            (4,),
            ((2, 3),),
            *gather(answers[h]),
            weights,
            acc3,
            mine,
            theirs,
            scratch=[VMEM((4 * size, cols), BF16), VMEM((4, size, cols), F32)],
        )
        got[h] = spread(outs[h])
    (turned,) = call(
        turned_kernel,
        [((3, 4, part, width), BF16)],
        turned0,
        turned1,
        *turned2.values(),
    )
    turned = after(turned, *got[CHUNKS - 1])[0]
    forest_out = lax.ppermute(turned, both, back)
    parts = []
    for h in every:
        parts += [outs[h][0], *got[h]]
    copies = 2 if layers == 2 else 1
    (total,) = call(
        run(total_kernel, CHUNKS),
        [((copies, 4, part, width), BF16 if copies == 2 else F32)],
        *parts,
    )
    if copies == 2:
        total = total.reshape(8, part, width)
        pieces = lax.all_to_all(total, ("layer", "prow"), 0, 0, tiled=True)
        pieces = pieces.reshape(2, 4, part, width)
        (root_out,) = call(join_kernel, [piece], pieces)
    else:
        total = lax.psum(total[0], "layer")
        root_out = lax.all_to_all(total, "prow", 0, 0, tiled=True).astype(BF16)
    return forest_out.reshape(1, 3 * size, width), root_out.reshape(size, width)


def solution(mesh):
    placed = (
        P("layer", ("prow", "pcol"), None),
        P(("prow", "pcol"), None),
        P("layer", None, "prow", "pcol", None, None, None, None),
        P("layer", None, "prow", "pcol", None, None),
        P("layer", None, "prow", "pcol", None, None),
        P("prow", "pcol", None, None),
    )
    return jax.shard_map(
        shards,
        mesh=mesh,
        in_specs=placed,
        out_specs=(P("layer", ("prow", "pcol"), None), P(("prow", "pcol"), None)),
        check_vma=False,
    )
```

```python
import functools

import jax
import jax.numpy as jnp
from jax import lax
from jax.experimental import pallas as pl
from jax.experimental.pallas import tpu as pltpu
from jax.sharding import PartitionSpec as P

F32 = jnp.float32
BF16 = jnp.bfloat16
VMEM = pltpu.VMEM
MIB = 1024 * 1024
LARGE = 60
CHUNKS = 2


def whole(count):
    return [pl.BlockSpec(memory_space=VMEM)] * count


def cost(micros):
    return pl.CostEstimate(
        flops=0, bytes_accessed=int(micros * 3.69e6), transcendentals=0
    )


def call(kernel, outs, *args, scratch=(), in_specs=None, limit=32, time=0.1):
    return pl.pallas_call(
        kernel,
        out_shape=[jax.ShapeDtypeStruct(shape, dtype) for shape, dtype in outs],
        in_specs=whole(len(args)) if in_specs is None else in_specs,
        out_specs=whole(len(outs)),
        scratch_shapes=list(scratch),
        compiler_params=pltpu.CompilerParams(vmem_limit_bytes=limit * MIB),
        cost_estimate=cost(time),
    )(*args)


def dot(left, right):
    return jnp.dot(left, right, preferred_element_type=F32)


def split(value):
    high = value.astype(BF16)
    return high, (value - high.astype(F32)).astype(BF16)


def precise(inverse, value):
    ih, il = inverse
    vh, vl = split(value)
    return dot(
        jnp.concatenate([ih, ih, il], axis=1), jnp.concatenate([vh, vl, vh], axis=0)
    )


def packed(inverse):
    high, low = split(inverse)
    half = high.shape[0] // 2
    return jnp.concatenate([high[:half], high[half:], low[:half], low[half:]], axis=1)


def unpacked(value):
    size = value.shape[1] // 4
    parts = [value[:, i * size : (i + 1) * size] for i in range(4)]
    return (
        jnp.concatenate(parts[:2], axis=0),
        jnp.concatenate(parts[2:], axis=0),
    )


def here():
    a, b = lax.axis_index("prow"), lax.axis_index("pcol")
    return a, b, a % 2


def at(start, length):
    return pl.ds(pl.multiple_of(start * length, length), length)


def crossed(index):
    return 2 * (index % 2) + index // 2


def pack_kernel(forest, root, inverses, last, side, own, near, far, *rest):
    held, top, inverse, final, sems = rest
    a, b, _ = here()
    part, wide = held.shape[2], side.shape[-1]
    half = final.shape[0] // 2
    moves = [
        pltpu.make_async_copy(source, out, sems.at[i])
        for i, (source, out) in enumerate(
            (
                (forest, held),
                (inverses, inverse),
                (root, top),
                (last, final),
            )
        )
    ]
    for move in moves:
        move.start()

    def piece(rows, k):
        there = a ^ k
        base, columns = there - there % 2, at(there % 2, wide)
        return jnp.concatenate(
            [rows[base, :, columns], rows[base + 1, :, columns]], axis=1
        )

    moves[0].wait()
    for i in range(2):
        side[i] = held[0, :, :, at((b % 2) ^ i, wide)]
    for i in range(1, 4):
        moves[i].wait()
    for out, slots in ((own, (0,)), (near, (1,)), (far, (2, 3))):
        out[:half] = packed(inverse[0])
        start = half
        for k in slots:
            for rows in (held.at[1], held.at[2], top):
                out[start : start + part] = piece(rows, k)
                start += part
    for value in (inverse[1], inverse[2], final[...]):
        for out in (own, near):
            out[start - 3 * part : start - 3 * part + half] = packed(value)
        start += half


def masked_rows(n, pattern, block, out, index):
    b, base = lax.axis_index("pcol"), index - index % 2
    size = block.shape[-1]
    for j in range(4):
        for k in range(4):
            value = block[b ^ j, base ^ k]
            out[j, :, k * size : (k + 1) * size] = jnp.where(
                pattern[n, b ^ j, base ^ k] != 0, value, jnp.zeros_like(value)
            )


def mask_kernel(first, flip, pattern, blocks, out, held, sems):
    a, _, _ = here()
    moves = [
        pltpu.make_async_copy(blocks.at[first + n], held.at[n], sems.at[n])
        for n in range(out.shape[0])
    ]
    for move in moves:
        move.start()
    for n, move in enumerate(moves):
        move.wait()
        masked_rows(first + n, pattern, held.at[n], out.at[n], a ^ flip)


def products(weights, solved):
    four, size, depth = weights.shape
    value = dot(weights[...].reshape(four * size, depth), solved[...])
    return value.reshape(four, size, solved.shape[1])


def send_sums(acc, own, other, solved, o0, o2, message):
    _, _, c = here()
    rows, size = o0.shape[0], own.shape[1]
    for weights, r in ((own, c), (other, 1 - c)):
        value = acc[r] - products(weights, solved)
        o0[at(r, size)] = value[0]
        o2[at(r, size)] = value[2]
        message[at(r, size)] = value[3].astype(message.dtype)
        message[at(2 + r, size)] = value[1].astype(message.dtype)


def place_rows(acc, given, h):
    _, b, _ = here()
    part, cols = given.shape[2], acc.shape[-1]
    acc[...] = jnp.zeros_like(acc)
    value = given[:, :, :, h * cols : (h + 1) * cols]
    acc[:, :, at(b, part)] = value.astype(F32)


def first_kernel(g0, g1, g2, g3, m0, m1, m2, m3, own, other, *rest):
    *solved, given, o0, o2, message, rows, acc = rest
    a, b, c = here()
    part, cols = g0.shape[-2], o0.shape[-1]
    size = 4 * part
    half = size // 2
    for m, piece in enumerate((g0, g1, g2, g3)):
        for u in range(4):
            rows[u, at(a ^ m, part)] = piece[m % 2, u]
    for m, packet in enumerate((m0, m1, m2, m3)):
        high, low = unpacked(packet[:half])
        right = rows[a ^ m]
        answer = dot(
            jnp.concatenate([high, low], axis=1),
            jnp.concatenate([right, right], axis=0),
        ).astype(BF16)
        for h, out in enumerate(solved):
            out[at(m ^ c, size)] = answer[:, h * cols : (h + 1) * cols]
        start = half + (3 * part if m == 3 else 0)
        wide = given.shape[-1]
        for level in range(3):
            for r in range(2):
                value = packet[start : start + part, r * wide : (r + 1) * wide]
                given[level, r, a ^ b ^ m] = value
            start += part
    place_rows(acc, given.at[0], 0)
    send_sums(acc, own.at[0], other.at[0], solved[0], o0, o2, message)


def second_kernel(h, solved, given, own, other, o0, o2, message, acc):
    place_rows(acc, given.at[0], h)
    send_sums(acc, own.at[0], other.at[0], solved, o0, o2, message)


def add_kernel(kept, came, out):
    out[...] = (kept[...] + came[: kept.shape[0]].astype(F32)).astype(out.dtype)


def summed(terms):
    rows = terms[-1].shape[0]
    total = terms[0][...].astype(F32)
    for term in terms[1:]:
        total += term[term.shape[0] - rows :].astype(F32)
    return total


def sum_kernel(*refs):
    refs[-1][...] = summed(refs[:-1]).astype(refs[-1].dtype)


def solve_kernel(level, *refs):
    *terms, own, near, out, value = refs
    _, _, c = here()
    value[...] = summed(terms)
    size = value.shape[0] // 2
    half = size // 2
    start = near.shape[0] - (4 - level) * half
    for message, r in ((own, c), (near, 1 - c)):
        inverse = unpacked(message[start : start + half])
        out[at(r, size)] = precise(inverse, value[at(r, size)]).astype(out.dtype)


def middle_kernel(own_at, other_at, s, far, own, other, acc, solved, *outs):
    rows = s.shape[0]
    solved[:rows] = s[...]
    solved[rows:] = far[...]
    send_sums(acc, own.at[own_at], other.at[other_at], solved, *outs)


def turn_rows(solved, mine, theirs):
    a, _, c = here()
    part = mine.shape[1]
    for out, index in ((mine, crossed(a)), (theirs, crossed(a ^ 1))):
        for k in range(4):
            out[(a - c) ^ k] = solved[at(4 * k + index, part)]


def rows_kernel(solved, mine, theirs):
    turn_rows(solved, mine, theirs)


def early_kernel(h, solved, given, own, other, *outs):
    acc2, acc3, mine, theirs = outs
    _, _, c = here()
    turn_rows(solved, mine, theirs)
    top = (lax.axis_index("layer") == 0).astype(F32)
    place_rows(acc2, given.at[1], h)
    place_rows(acc3, given.at[2], h)
    acc3[...] *= top
    for r, weights, first in ((c, own, 1), (1 - c, other, 0)):
        acc2[r] -= products(weights.at[first], solved)
        acc3[r] -= products(weights.at[first + 1], solved)


def later_kernel(solved, own, other, acc, out, mine, theirs):
    _, _, c = here()
    turn_rows(solved, mine, theirs)
    out[c] = acc[c] - products(own.at[4], solved)
    out[1 - c] = acc[1 - c] - products(other.at[3], solved)


def turn_kernel(*refs):
    *parts, mine, theirs = refs
    cols = parts[0].shape[-1]
    for index in range(0, len(parts), 2):
        level, h = divmod(index // 2, CHUNKS)
        columns = slice(h * cols, (h + 1) * cols)
        mine[level, :, :, columns] = parts[index][...]
        theirs[level, :, :, columns] = parts[index + 1][...]


def last_kernel(*refs):
    *parts, mine, theirs = refs
    a, _, c = here()
    rows, cols = parts[0].shape
    part = mine.shape[2]
    for index, piece in enumerate(parts):
        h, group = divmod(index, 2)
        columns = slice(h * cols, (h + 1) * cols)
        for out, place in ((mine, crossed(a)), (theirs, crossed(a ^ 1))):
            for r in range(2):
                value = piece[at(4 * r + place, part)]
                out[0, (a - c) ^ (2 * group + r), :, columns] = value


def swap_kernel(mine, came, out):
    _, _, c = here()
    cols = came.shape[-1]
    for level in range(out.shape[0]):
        out[level, :, :, at(c, cols)] = mine[level]
        out[level, :, :, at(1 - c, cols)] = came[level]


def output_kernel(first, second, forest, root):
    forest[...] = first[...]
    root[...] = second[...]


def shards(subtree_right_hand, root_rhs, blocks, pattern, forest_inverse, root_inverse):
    layers = lax.axis_size("layer")
    size = blocks.shape[-1]
    part, half = size // 4, size // 2
    width = subtree_right_hand.shape[-1]
    forest = subtree_right_hand.reshape(3, 4, part, width)
    root = root_rhs.reshape(4, part, width)
    blocks = blocks.reshape(6, 4, 4, size, size)
    pattern = pattern.reshape(6, 4, 4)
    inverses = forest_inverse.reshape(3, size, size)
    last_inverse = root_inverse.reshape(size, size)
    both = ("prow", "pcol")
    turn = [(i * 4 + j, j * 4 + i) for i in range(4) for j in range(4)]
    back = [
        [(i * 4 + j, j * 4 + crossed(i ^ k)) for i in range(4) for j in range(4)]
        for k in range(2)
    ]
    hbm = pl.BlockSpec(memory_space=pltpu.HBM)
    dma = pltpu.SemaphoreType.DMA
    run = functools.partial

    def after(*values):
        return lax.optimization_barrier(values)

    def swap(value, axis, k):
        return lax.ppermute(value, axis, [(i, i ^ k) for i in range(4)])

    tokens = []

    def step(how, kernel, outs, *args, in_specs=None, **options):
        count = len(args)
        specs = whole(count) if in_specs is None else list(in_specs)
        chained = bool(tokens)

        def body(*refs):
            ins, refs = refs[:count], refs[count + chained :]
            made, token, held = refs[: len(outs)], refs[len(outs)], refs[len(outs) + 1 :]
            token[...] = jnp.zeros_like(token)
            kernel(*ins, *made, *held)

        *results, token = how(
            body,
            [*outs, ((8, 128), F32)],
            *args,
            *tokens,
            in_specs=specs + whole(chained),
            **options,
        )
        tokens[:] = [token]
        return results

    rows = 2 * size
    wide = width // 2
    cols = wide // CHUNKS
    every = range(CHUNKS)
    block, kept = ((rows, cols), BF16), ((rows, cols), F32)
    sums = ((2, 4, size, cols), F32)
    tall = ((4 * size, cols), BF16)
    turned = ((4, part, cols), BF16)

    side, own, near, far = call(
        pack_kernel,
        [
            ((2, 4, part, wide), BF16),
            ((4 * half + 3 * part, width), BF16),
            ((4 * half + 3 * part, width), BF16),
            ((half + 6 * part, width), BF16),
        ],
        forest,
        root,
        inverses,
        last_inverse,
        in_specs=[hbm] * 4,
        time=2,
        scratch=[
            VMEM((3, 4, part, width), BF16),
            VMEM((4, part, width), BF16),
            VMEM((3, size, size), F32),
            VMEM((size, size), F32),
            dma((4,)),
        ],
        limit=LARGE,
    )
    side = lax.ppermute(side, both, turn)
    far = swap(far, "prow", 2)
    near = swap(near, "prow", 1)
    blocks_other, pattern_other = swap(blocks, "prow", 1), swap(pattern, "prow", 1)
    smem = pl.BlockSpec(memory_space=pltpu.SMEM)

    def masked(first, count, flip):
        (out,) = step(
            call,
            run(mask_kernel, first, flip),
            [((count, 4, size, 4 * size), BF16)],
            pattern_other if flip else pattern,
            blocks_other if flip else blocks,
            in_specs=[smem, hbm],
            scratch=[VMEM((count, 4, 4, size, size), BF16), dma((count,))],
            time=0.3 * count,
        )
        return out

    weights = masked(0, 6, 0)
    side, far, weights = after(side, far, weights)
    fourth = swap(far, "prow", 1)

    def send(outs):
        return swap(outs[2], "pcol", 1)

    def add(outs, came):
        (passed,) = step(call, add_kernel, [block], outs[1], came)
        return outs[0], came, swap(passed, "pcol", 2)

    def solve(level, *terms):
        (answer,) = step(
            call,
            run(solve_kernel, level),
            [block],
            *terms,
            own,
            near,
            scratch=[VMEM(*kept)],
            time=0.3,
        )
        return answer, swap(answer, "prow", 2)

    def join(mine, theirs):
        shape = (mine.shape[0], 4, part, width)
        return step(call, swap_kernel, [(shape, BF16)], mine, theirs)[0]

    message = ((2 * rows, cols), BF16)
    cross = swap(side, "prow", 2)
    sides = (side, swap(side, "prow", 1), cross, swap(cross, "prow", 1))
    first_other = masked(0, 1, 1)
    solved, outs, came, terms, pieces, acc2, acc3 = ({} for _ in range(7))
    turns = [{}, {}, {}]

    def early(h):
        acc2[h], acc3[h], *turns[0][h] = step(
            call,
            run(early_kernel, h),
            [sums, sums, turned, turned],
            solved[h],
            given,
            weights,
            others,
            time=0.7,
        )

    def later(h):
        acc3[h], *turns[1][h] = step(
            call,
            later_kernel,
            [sums, turned, turned],
            solved[h],
            weights,
            others,
            acc3[h],
            time=0.4,
        )

    def middle(h, pair, acc):
        solved[h], *outs[h] = step(
            call,
            run(middle_kernel, pair, pair - 1),
            [tall, kept, kept, message],
            *pieces[h],
            weights,
            others,
            acc[h],
            time=0.4,
        )
        came[h] = send(outs[h])

    *values, given, o0, o2, first_message = step(
        call,
        first_kernel,
        [tall] * CHUNKS + [((3, 2, 4, part, wide), BF16), kept, kept, message],
        *sides,
        own,
        near,
        far,
        fourth,
        weights,
        first_other,
        scratch=[VMEM((4, size, wide), BF16), VMEM((2, 4, size, cols), F32)],
        time=1.5,
    )
    for h in every:
        solved[h] = values[h]
        if h > 0:
            o0, o2, first_message = step(
                call,
                run(second_kernel, h),
                [kept, kept, message],
                solved[h],
                given,
                weights,
                first_other,
                scratch=[VMEM((2, 4, size, cols), F32)],
                time=0.4,
            )
        outs[h] = o0, o2, first_message
        came[h] = send(outs[h])
    others = masked(1, 5, 1)
    for h in every:
        terms[h] = add(outs[h], came[h])
        early(h)
    for h in every:
        pieces[h] = solve(1, *terms[h])
    for h in every:
        middle(h, 3, acc2)
    for h in every:
        terms[h] = add(outs[h], came[h])
        later(h)
    for h in every:
        pieces[h] = solve(2, *terms[h])
    for h in every:
        middle(h, 5, acc3)
    for h in every:
        turns[2][h] = step(call, rows_kernel, [turned, turned], solved[h])
    parts = [value for level in turns for h in every for value in level[h]]
    mine, theirs = step(call, turn_kernel, [((3, 4, part, wide), BF16)] * 2, *parts)
    theirs = swap(theirs, "prow", 1)
    for h in every:
        terms[h] = add(outs[h], came[h])
        if h == 0:
            pass
    for h in every:
        if h == 1:
            forest_rows = join(mine, theirs)
        (total,) = step(call, sum_kernel, [block if layers == 2 else kept], *terms[h])
        if layers == 2:
            terms[h] = total, lax.ppermute(total, "layer", [(0, 1), (1, 0)])
        else:
            terms[h] = (lax.psum(total, "layer"),)
    forest_out = lax.ppermute(forest_rows, both, back[0])
    for h in every:
        pieces[h] = solve(3, *terms[h])
    lasts = [piece for h in every for piece in pieces[h]]
    mine, theirs = step(call, last_kernel, [((1, 4, part, wide), BF16)] * 2, *lasts)
    root_rows = join(mine, swap(theirs, "prow", 1))
    root_out = lax.ppermute(root_rows, both, back[0])
    forest_out, root_out = step(
        call,
        output_kernel,
        [((3, 4, part, width), BF16), ((1, 4, part, width), BF16)],
        forest_out,
        root_out,
    )
    return forest_out.reshape(1, 3 * size, width), root_out.reshape(size, width)


def solution(mesh):
    placed = (
        P("layer", ("prow", "pcol"), None),
        P(("prow", "pcol"), None),
        P("layer", None, "prow", "pcol", None, None, None, None),
        P("layer", None, "prow", "pcol", None, None),
        P("layer", None, "prow", "pcol", None, None),
        P("prow", "pcol", None, None),
    )
    return jax.shard_map(
        shards,
        mesh=mesh,
        in_specs=placed,
        out_specs=(P("layer", ("prow", "pcol"), None), P(("prow", "pcol"), None)),
        check_vma=False,
    )
```

```python
import functools

import jax
import jax.numpy as jnp
from jax import lax
from jax.experimental import pallas as pl
from jax.experimental.pallas import tpu as pltpu
from jax.sharding import PartitionSpec as P

F32 = jnp.float32
BF16 = jnp.bfloat16
VMEM = pltpu.VMEM
MIB = 1024 * 1024
LARGE = 60
CHUNKS = 2


def whole(count):
    return [pl.BlockSpec(memory_space=VMEM)] * count


def cost(micros):
    return pl.CostEstimate(
        flops=0, bytes_accessed=int(micros * 3.69e6), transcendentals=0
    )


def call(kernel, outs, *args, scratch=(), in_specs=None, limit=32, time=0.1):
    return pl.pallas_call(
        kernel,
        out_shape=[jax.ShapeDtypeStruct(shape, dtype) for shape, dtype in outs],
        in_specs=whole(len(args)) if in_specs is None else in_specs,
        out_specs=whole(len(outs)),
        scratch_shapes=list(scratch),
        compiler_params=pltpu.CompilerParams(vmem_limit_bytes=limit * MIB),
        cost_estimate=cost(time),
    )(*args)


def dot(left, right):
    return jnp.dot(left, right, preferred_element_type=F32)


def split(value):
    high = value.astype(BF16)
    return high, (value - high.astype(F32)).astype(BF16)


def precise(inverse, value):
    ih, il = inverse
    vh, vl = split(value)
    return dot(
        jnp.concatenate([ih, ih, il], axis=1), jnp.concatenate([vh, vl, vh], axis=0)
    )


def packed(inverse):
    high, low = split(inverse)
    half = high.shape[0] // 2
    return jnp.concatenate([high[:half], high[half:], low[:half], low[half:]], axis=1)


def unpacked(value):
    size = value.shape[1] // 4
    parts = [value[:, i * size : (i + 1) * size] for i in range(4)]
    return (
        jnp.concatenate(parts[:2], axis=0),
        jnp.concatenate(parts[2:], axis=0),
    )


def here():
    a, b = lax.axis_index("prow"), lax.axis_index("pcol")
    return a, b, a % 2


def at(start, length):
    return pl.ds(pl.multiple_of(start * length, length), length)


def crossed(index):
    return (4 - index) % 4


def pack_kernel(forest, root, inverses, last, side, own, near, far, *rest):
    held, top, inverse, final, sems = rest
    a, b, _ = here()
    part, wide = held.shape[2], side.shape[-1]
    half = final.shape[0] // 2
    moves = [
        pltpu.make_async_copy(source, out, sems.at[i])
        for i, (source, out) in enumerate(
            (
                (forest, held),
                (inverses, inverse),
                (root, top),
                (last, final),
            )
        )
    ]
    for move in moves:
        move.start()

    def piece(rows, k):
        there = a ^ k
        base, columns = there - there % 2, at(there % 2, wide)
        return jnp.concatenate(
            [rows[base, :, columns], rows[base + 1, :, columns]], axis=1
        )

    moves[0].wait()
    for i in range(2):
        side[i] = held[0, :, :, at((b % 2) ^ i, wide)]
    for i in range(1, 4):
        moves[i].wait()
    for out, slots in ((own, (0,)), (near, (1,)), (far, (2, 3))):
        out[:half] = packed(inverse[0])
        start = half
        for k in slots:
            for rows in (held.at[1], held.at[2], top):
                out[start : start + part] = piece(rows, k)
                start += part
    for value in (inverse[1], inverse[2], final[...]):
        for out in (own, near):
            out[start - 3 * part : start - 3 * part + half] = packed(value)
        start += half


def masked_rows(n, pattern, block, out, index):
    b, base = lax.axis_index("pcol"), index - index % 2
    size = block.shape[-1]
    for j in range(4):
        for k in range(4):
            value = block[b ^ j, base ^ k]
            out[j, :, k * size : (k + 1) * size] = jnp.where(
                pattern[n, b ^ j, base ^ k] != 0, value, jnp.zeros_like(value)
            )


def mask_kernel(first, flip, pattern, blocks, out, held, sems):
    a, _, _ = here()
    moves = [
        pltpu.make_async_copy(blocks.at[first + n], held.at[n], sems.at[n])
        for n in range(out.shape[0])
    ]
    for move in moves:
        move.start()
    for n, move in enumerate(moves):
        move.wait()
        masked_rows(first + n, pattern, held.at[n], out.at[n], a ^ flip)


def products(weights, solved):
    four, size, depth = weights.shape
    value = dot(weights[...].reshape(four * size, depth), solved[...])
    return value.reshape(four, size, solved.shape[1])


def send_sums(acc, own, other, solved, o0, o2, message):
    _, _, c = here()
    rows, size = o0.shape[0], own.shape[1]
    for weights, r in ((own, c), (other, 1 - c)):
        value = acc[r] - products(weights, solved)
        o0[at(r, size)] = value[0]
        o2[at(r, size)] = value[2]
        message[at(r, size)] = value[3].astype(message.dtype)
        message[at(2 + r, size)] = value[1].astype(message.dtype)


def place_rows(acc, given, h):
    _, b, _ = here()
    part, cols = given.shape[2], acc.shape[-1]
    acc[...] = jnp.zeros_like(acc)
    value = given[:, :, :, h * cols : (h + 1) * cols]
    acc[:, :, at(b, part)] = value.astype(F32)


def first_kernel(g0, g1, g2, g3, m0, m1, m2, m3, own, other, *rest):
    *solved, given, o0, o2, message, rows, acc = rest
    a, b, c = here()
    part, cols = g0.shape[-2], o0.shape[-1]
    size = 4 * part
    half = size // 2
    for m, piece in enumerate((g0, g1, g2, g3)):
        for u in range(4):
            rows[u, at(a ^ m, part)] = piece[m % 2, u]
    for m, packet in enumerate((m0, m1, m2, m3)):
        high, low = unpacked(packet[:half])
        right = rows[a ^ m]
        answer = dot(
            jnp.concatenate([high, low], axis=1),
            jnp.concatenate([right, right], axis=0),
        ).astype(BF16)
        for h, out in enumerate(solved):
            out[at(m ^ c, size)] = answer[:, h * cols : (h + 1) * cols]
        start = half + (3 * part if m == 3 else 0)
        wide = given.shape[-1]
        for level in range(3):
            for r in range(2):
                value = packet[start : start + part, r * wide : (r + 1) * wide]
                given[level, r, a ^ b ^ m] = value
            start += part
    place_rows(acc, given.at[0], 0)
    send_sums(acc, own.at[0], other.at[0], solved[0], o0, o2, message)


def second_kernel(h, solved, given, own, other, o0, o2, message, acc):
    place_rows(acc, given.at[0], h)
    send_sums(acc, own.at[0], other.at[0], solved, o0, o2, message)


def add_kernel(kept, came, out):
    out[...] = (kept[...] + came[: kept.shape[0]].astype(F32)).astype(out.dtype)


def summed(terms):
    rows = terms[-1].shape[0]
    total = terms[0][...].astype(F32)
    for term in terms[1:]:
        total += term[term.shape[0] - rows :].astype(F32)
    return total


def sum_kernel(*refs):
    refs[-1][...] = summed(refs[:-1]).astype(refs[-1].dtype)


def solve_kernel(level, *refs):
    *terms, own, near, out, value = refs
    _, _, c = here()
    value[...] = summed(terms)
    size = value.shape[0] // 2
    half = size // 2
    start = near.shape[0] - (4 - level) * half
    for message, r in ((own, c), (near, 1 - c)):
        inverse = unpacked(message[start : start + half])
        out[at(r, size)] = precise(inverse, value[at(r, size)]).astype(out.dtype)


def middle_kernel(own_at, other_at, s, far, own, other, acc, solved, *outs):
    rows = s.shape[0]
    solved[:rows] = s[...]
    solved[rows:] = far[...]
    send_sums(acc, own.at[own_at], other.at[other_at], solved, *outs)


def turn_rows(solved, mine, theirs):
    a, _, c = here()
    part = mine.shape[1]
    for out, index in ((mine, crossed(a)), (theirs, crossed(a ^ 1))):
        for k in range(4):
            out[(a - c) ^ k] = solved[at(4 * k + index, part)]


def rows_kernel(solved, mine, theirs):
    turn_rows(solved, mine, theirs)


def early_kernel(h, solved, given, own, other, *outs):
    acc2, acc3, mine, theirs = outs
    _, _, c = here()
    turn_rows(solved, mine, theirs)
    top = (lax.axis_index("layer") == 0).astype(F32)
    place_rows(acc2, given.at[1], h)
    place_rows(acc3, given.at[2], h)
    acc3[...] *= top
    for r, weights, first in ((c, own, 1), (1 - c, other, 0)):
        acc2[r] -= products(weights.at[first], solved)
        acc3[r] -= products(weights.at[first + 1], solved)


def later_kernel(solved, own, other, acc, out, mine, theirs):
    _, _, c = here()
    turn_rows(solved, mine, theirs)
    out[c] = acc[c] - products(own.at[4], solved)
    out[1 - c] = acc[1 - c] - products(other.at[3], solved)


def turn_kernel(*refs):
    *parts, mine, theirs = refs
    cols = parts[0].shape[-1]
    for index in range(0, len(parts), 2):
        level, h = divmod(index // 2, CHUNKS)
        columns = slice(h * cols, (h + 1) * cols)
        mine[level, :, :, columns] = parts[index][...]
        theirs[level, :, :, columns] = parts[index + 1][...]


def last_kernel(*refs):
    *parts, mine, theirs = refs
    a, _, c = here()
    rows, cols = parts[0].shape
    part = mine.shape[2]
    for index, piece in enumerate(parts):
        h, group = divmod(index, 2)
        columns = slice(h * cols, (h + 1) * cols)
        for out, place in ((mine, crossed(a)), (theirs, crossed(a ^ 1))):
            for r in range(2):
                value = piece[at(4 * r + place, part)]
                out[0, (a - c) ^ (2 * group + r), :, columns] = value


def swap_kernel(mine, came, out):
    _, _, c = here()
    cols = came.shape[-1]
    for level in range(out.shape[0]):
        out[level, :, :, at(c, cols)] = mine[level]
        out[level, :, :, at(1 - c, cols)] = came[level]


def output_kernel(first, second, forest, root):
    forest[...] = first[...]
    root[...] = second[...]


def shards(subtree_right_hand, root_rhs, blocks, pattern, forest_inverse, root_inverse):
    layers = lax.axis_size("layer")
    size = blocks.shape[-1]
    part, half = size // 4, size // 2
    width = subtree_right_hand.shape[-1]
    forest = subtree_right_hand.reshape(3, 4, part, width)
    root = root_rhs.reshape(4, part, width)
    blocks = blocks.reshape(6, 4, 4, size, size)
    pattern = pattern.reshape(6, 4, 4)
    inverses = forest_inverse.reshape(3, size, size)
    last_inverse = root_inverse.reshape(size, size)
    both = ("prow", "pcol")
    turn = [(i * 4 + j, j * 4 + i) for i in range(4) for j in range(4)]
    back = [
        [(i * 4 + j, j * 4 + crossed(i ^ k)) for i in range(4) for j in range(4)]
        for k in range(2)
    ]
    hbm = pl.BlockSpec(memory_space=pltpu.HBM)
    dma = pltpu.SemaphoreType.DMA
    run = functools.partial

    def after(*values):
        return lax.optimization_barrier(values)

    def swap(value, axis, k):
        return lax.ppermute(value, axis, [(i, i ^ k) for i in range(4)])

    tokens = []

    def step(how, kernel, outs, *args, in_specs=None, **options):
        count = len(args)
        specs = whole(count) if in_specs is None else list(in_specs)
        chained = bool(tokens)

        def body(*refs):
            ins, refs = refs[:count], refs[count + chained :]
            made, token, held = refs[: len(outs)], refs[len(outs)], refs[len(outs) + 1 :]
            token[...] = jnp.zeros_like(token)
            kernel(*ins, *made, *held)

        *results, token = how(
            body,
            [*outs, ((8, 128), F32)],
            *args,
            *tokens,
            in_specs=specs + whole(chained),
            **options,
        )
        tokens[:] = [token]
        return results

    rows = 2 * size
    wide = width // 2
    cols = wide // CHUNKS
    every = range(CHUNKS)
    block, kept = ((rows, cols), BF16), ((rows, cols), F32)
    sums = ((2, 4, size, cols), F32)
    tall = ((4 * size, cols), BF16)
    turned = ((4, part, cols), BF16)

    side, own, near, far = call(
        pack_kernel,
        [
            ((2, 4, part, wide), BF16),
            ((4 * half + 3 * part, width), BF16),
            ((4 * half + 3 * part, width), BF16),
            ((half + 6 * part, width), BF16),
        ],
        forest,
        root,
        inverses,
        last_inverse,
        in_specs=[hbm] * 4,
        time=2,
        scratch=[
            VMEM((3, 4, part, width), BF16),
            VMEM((4, part, width), BF16),
            VMEM((3, size, size), F32),
            VMEM((size, size), F32),
            dma((4,)),
        ],
        limit=LARGE,
    )
    side = lax.ppermute(side, both, turn)
    far = swap(far, "prow", 2)
    near = swap(near, "prow", 1)
    blocks_other, pattern_other = swap(blocks, "prow", 1), swap(pattern, "prow", 1)
    smem = pl.BlockSpec(memory_space=pltpu.SMEM)

    def masked(first, count, flip):
        (out,) = step(
            call,
            run(mask_kernel, first, flip),
            [((count, 4, size, 4 * size), BF16)],
            pattern_other if flip else pattern,
            blocks_other if flip else blocks,
            in_specs=[smem, hbm],
            scratch=[VMEM((count, 4, 4, size, size), BF16), dma((count,))],
            time=0.3 * count,
        )
        return out

    weights = masked(0, 6, 0)
    side, far, weights = after(side, far, weights)
    fourth = swap(far, "prow", 1)

    def send(outs):
        return swap(outs[2], "pcol", 1)

    def add(outs, came):
        (passed,) = step(call, add_kernel, [block], outs[1], came)
        return outs[0], came, swap(passed, "pcol", 2)

    def solve(level, *terms):
        (answer,) = step(
            call,
            run(solve_kernel, level),
            [block],
            *terms,
            own,
            near,
            scratch=[VMEM(*kept)],
            time=0.3,
        )
        return answer, swap(answer, "prow", 2)

    def join(mine, theirs):
        shape = (mine.shape[0], 4, part, width)
        return step(call, swap_kernel, [(shape, BF16)], mine, theirs)[0]

    message = ((2 * rows, cols), BF16)
    cross = swap(side, "prow", 2)
    sides = (side, swap(side, "prow", 1), cross, swap(cross, "prow", 1))
    first_other = masked(0, 1, 1)
    solved, outs, came, terms, pieces, acc2, acc3 = ({} for _ in range(7))
    turns = [{}, {}, {}]

    def early(h):
        acc2[h], acc3[h], *turns[0][h] = step(
            call,
            run(early_kernel, h),
            [sums, sums, turned, turned],
            solved[h],
            given,
            weights,
            others,
            time=0.7,
        )

    def later(h):
        acc3[h], *turns[1][h] = step(
            call,
            later_kernel,
            [sums, turned, turned],
            solved[h],
            weights,
            others,
            acc3[h],
            time=0.4,
        )

    def middle(h, pair, acc):
        solved[h], *outs[h] = step(
            call,
            run(middle_kernel, pair, pair - 1),
            [tall, kept, kept, message],
            *pieces[h],
            weights,
            others,
            acc[h],
            time=0.4,
        )
        came[h] = send(outs[h])

    *values, given, o0, o2, first_message = step(
        call,
        first_kernel,
        [tall] * CHUNKS + [((3, 2, 4, part, wide), BF16), kept, kept, message],
        *sides,
        own,
        near,
        far,
        fourth,
        weights,
        first_other,
        scratch=[VMEM((4, size, wide), BF16), VMEM((2, 4, size, cols), F32)],
        time=1.5,
    )
    for h in every:
        solved[h] = values[h]
        if h > 0:
            o0, o2, first_message = step(
                call,
                run(second_kernel, h),
                [kept, kept, message],
                solved[h],
                given,
                weights,
                first_other,
                scratch=[VMEM((2, 4, size, cols), F32)],
                time=0.4,
            )
        outs[h] = o0, o2, first_message
        came[h] = send(outs[h])
    others = masked(1, 5, 1)
    for h in every:
        terms[h] = add(outs[h], came[h])
    for h in every:
        early(h)
    for h in every:
        pieces[h] = solve(1, *terms[h])
    for h in every:
        middle(h, 3, acc2)
    for h in every:
        terms[h] = add(outs[h], came[h])
    for h in every:
        later(h)
    for h in every:
        pieces[h] = solve(2, *terms[h])
    for h in every:
        middle(h, 5, acc3)
    for h in every:
        turns[2][h] = step(call, rows_kernel, [turned, turned], solved[h])
    parts = [value for level in turns for h in every for value in level[h]]
    mine, theirs = step(call, turn_kernel, [((3, 4, part, wide), BF16)] * 2, *parts)
    theirs = swap(theirs, "prow", 1)
    for h in every:
        terms[h] = add(outs[h], came[h])
        if h == 0:
            pass
    for h in every:
        if h == 1:
            forest_rows = join(mine, theirs)
        (total,) = step(call, sum_kernel, [block if layers == 2 else kept], *terms[h])
        if layers == 2:
            terms[h] = total, lax.ppermute(total, "layer", [(0, 1), (1, 0)])
        else:
            terms[h] = (lax.psum(total, "layer"),)
    forest_out = lax.ppermute(forest_rows, both, back[0])
    for h in every:
        pieces[h] = solve(3, *terms[h])
    lasts = [piece for h in every for piece in pieces[h]]
    mine, theirs = step(call, last_kernel, [((1, 4, part, wide), BF16)] * 2, *lasts)
    root_rows = join(mine, swap(theirs, "prow", 1))
    root_out = lax.ppermute(root_rows, both, back[0])
    forest_out, root_out = step(
        call,
        output_kernel,
        [((3, 4, part, width), BF16), ((1, 4, part, width), BF16)],
        forest_out,
        root_out,
    )
    return forest_out.reshape(1, 3 * size, width), root_out.reshape(size, width)


def solution(mesh):
    placed = (
        P("layer", ("prow", "pcol"), None),
        P(("prow", "pcol"), None),
        P("layer", None, "prow", "pcol", None, None, None, None),
        P("layer", None, "prow", "pcol", None, None),
        P("layer", None, "prow", "pcol", None, None),
        P("prow", "pcol", None, None),
    )
    return jax.shard_map(
        shards,
        mesh=mesh,
        in_specs=placed,
        out_specs=(P("layer", ("prow", "pcol"), None), P(("prow", "pcol"), None)),
        check_vma=False,
    )
```

```python
import functools

import jax
import jax.numpy as jnp
from jax import lax
from jax.experimental import pallas as pl
from jax.experimental.pallas import tpu as pltpu
from jax.sharding import PartitionSpec as P

F32 = jnp.float32
BF16 = jnp.bfloat16
VMEM = pltpu.VMEM
MIB = 1024 * 1024
LARGE = 60
CHUNKS = 2


def whole(count):
    return [pl.BlockSpec(memory_space=VMEM)] * count


def cost(micros):
    return pl.CostEstimate(
        flops=0, bytes_accessed=int(micros * 3.69e6), transcendentals=0
    )


def call(kernel, outs, *args, scratch=(), in_specs=None, limit=32, time=0.1):
    return pl.pallas_call(
        kernel,
        out_shape=[jax.ShapeDtypeStruct(shape, dtype) for shape, dtype in outs],
        in_specs=whole(len(args)) if in_specs is None else in_specs,
        out_specs=whole(len(outs)),
        scratch_shapes=list(scratch),
        compiler_params=pltpu.CompilerParams(vmem_limit_bytes=limit * MIB),
        cost_estimate=cost(time),
    )(*args)


def dot(left, right):
    return jnp.dot(left, right, preferred_element_type=F32)


def split(value):
    high = value.astype(BF16)
    return high, (value - high.astype(F32)).astype(BF16)


def precise(inverse, value):
    ih, il = inverse
    vh, vl = split(value)
    return dot(
        jnp.concatenate([ih, ih, il], axis=1), jnp.concatenate([vh, vl, vh], axis=0)
    )


def packed(inverse):
    high, low = split(inverse)
    half = high.shape[0] // 2
    return jnp.concatenate([high[:half], high[half:], low[:half], low[half:]], axis=1)


def unpacked(value):
    size = value.shape[1] // 4
    parts = [value[:, i * size : (i + 1) * size] for i in range(4)]
    return (
        jnp.concatenate(parts[:2], axis=0),
        jnp.concatenate(parts[2:], axis=0),
    )


def here():
    a, b = lax.axis_index("prow"), lax.axis_index("pcol")
    return a, b, a % 2


def at(start, length):
    return pl.ds(pl.multiple_of(start * length, length), length)


def crossed(index):
    return (4 - index) % 4


def pack_kernel(forest, root, inverses, last, side, own, near, far, *rest):
    held, top, inverse, final, sems = rest
    a, b, _ = here()
    part, wide = held.shape[2], side.shape[-1]
    half = final.shape[0] // 2
    moves = [
        pltpu.make_async_copy(source, out, sems.at[i])
        for i, (source, out) in enumerate(
            (
                (forest, held),
                (inverses, inverse),
                (root, top),
                (last, final),
            )
        )
    ]
    for move in moves:
        move.start()

    def piece(rows, k):
        there = a ^ k
        base, columns = there - there % 2, at(there % 2, wide)
        return jnp.concatenate(
            [rows[base, :, columns], rows[base + 1, :, columns]], axis=1
        )

    moves[0].wait()
    for i in range(2):
        side[i] = held[0, :, :, at((b % 2) ^ i, wide)]
    for i in range(1, 4):
        moves[i].wait()
    for out, slots in ((own, (0,)), (near, (1,)), (far, (2, 3))):
        out[:half] = packed(inverse[0])
        start = half
        for k in slots:
            for rows in (held.at[1], held.at[2], top):
                out[start : start + part] = piece(rows, k)
                start += part
    for value in (inverse[1], inverse[2], final[...]):
        for out in (own, near):
            out[start - 3 * part : start - 3 * part + half] = packed(value)
        start += half


def masked_rows(n, pattern, block, out, index):
    b, base = lax.axis_index("pcol"), index - index % 2
    size = block.shape[-1]
    for j in range(4):
        for k in range(4):
            value = block[b ^ j, base ^ k]
            out[j, :, k * size : (k + 1) * size] = jnp.where(
                pattern[n, b ^ j, base ^ k] != 0, value, jnp.zeros_like(value)
            )


def mask_kernel(first, flip, pattern, blocks, out, held, sems):
    a, _, _ = here()
    moves = [
        pltpu.make_async_copy(blocks.at[first + n], held.at[n], sems.at[n])
        for n in range(out.shape[0])
    ]
    for move in moves:
        move.start()
    for n, move in enumerate(moves):
        move.wait()
        masked_rows(first + n, pattern, held.at[n], out.at[n], a ^ flip)


def products(weights, solved):
    four, size, depth = weights.shape
    value = dot(weights[...].reshape(four * size, depth), solved[...])
    return value.reshape(four, size, solved.shape[1])


def send_sums(acc, own, other, solved, o0, o2, message):
    _, _, c = here()
    rows, size = o0.shape[0], own.shape[1]
    for weights, r in ((own, c), (other, 1 - c)):
        value = acc[r] - products(weights, solved)
        o0[at(r, size)] = value[0]
        o2[at(r, size)] = value[2]
        message[at(r, size)] = value[3].astype(message.dtype)
        message[at(2 + r, size)] = value[1].astype(message.dtype)


def place_rows(acc, given, h):
    _, b, _ = here()
    part, cols = given.shape[2], acc.shape[-1]
    acc[...] = jnp.zeros_like(acc)
    value = given[:, :, :, h * cols : (h + 1) * cols]
    acc[:, :, at(b, part)] = value.astype(F32)


def first_kernel(g0, g1, g2, g3, m0, m1, m2, m3, own, other, *rest):
    *solved, given, o0, o2, message, rows, acc = rest
    a, b, c = here()
    part, cols = g0.shape[-2], o0.shape[-1]
    size = 4 * part
    half = size // 2
    for m, piece in enumerate((g0, g1, g2, g3)):
        for u in range(4):
            rows[u, at(a ^ m, part)] = piece[m % 2, u]
    for m, packet in enumerate((m0, m1, m2, m3)):
        high, low = unpacked(packet[:half])
        right = rows[a ^ m]
        answer = dot(
            jnp.concatenate([high, low], axis=1),
            jnp.concatenate([right, right], axis=0),
        ).astype(BF16)
        for h, out in enumerate(solved):
            out[at(m ^ c, size)] = answer[:, h * cols : (h + 1) * cols]
        start = half + (3 * part if m == 3 else 0)
        wide = given.shape[-1]
        for level in range(3):
            for r in range(2):
                value = packet[start : start + part, r * wide : (r + 1) * wide]
                given[level, r, a ^ b ^ m] = value
            start += part
    place_rows(acc, given.at[0], 0)
    send_sums(acc, own.at[0], other.at[0], solved[0], o0, o2, message)


def second_kernel(h, solved, given, own, other, o0, o2, message, acc):
    place_rows(acc, given.at[0], h)
    send_sums(acc, own.at[0], other.at[0], solved, o0, o2, message)


def add_kernel(kept, came, out):
    out[...] = (kept[...] + came[: kept.shape[0]].astype(F32)).astype(out.dtype)


def summed(terms):
    rows = terms[-1].shape[0]
    total = terms[0][...].astype(F32)
    for term in terms[1:]:
        total += term[term.shape[0] - rows :].astype(F32)
    return total


def sum_kernel(*refs):
    refs[-1][...] = summed(refs[:-1]).astype(refs[-1].dtype)


def solve_kernel(level, *refs):
    *terms, own, near, out, value = refs
    _, _, c = here()
    value[...] = summed(terms)
    size = value.shape[0] // 2
    half = size // 2
    start = near.shape[0] - (4 - level) * half
    for message, r in ((own, c), (near, 1 - c)):
        inverse = unpacked(message[start : start + half])
        out[at(r, size)] = precise(inverse, value[at(r, size)]).astype(out.dtype)


def middle_kernel(own_at, other_at, s, far, own, other, acc, solved, *outs):
    rows = s.shape[0]
    solved[:rows] = s[...]
    solved[rows:] = far[...]
    send_sums(acc, own.at[own_at], other.at[other_at], solved, *outs)


def turn_rows(solved, mine, theirs):
    a, _, c = here()
    part = mine.shape[1]
    for out, index in ((mine, crossed(a)), (theirs, crossed(a ^ 1))):
        for k in range(4):
            out[(a - c) ^ k] = solved[at(4 * k + index, part)]


def rows_kernel(solved, mine, theirs):
    turn_rows(solved, mine, theirs)


def early_kernel(h, solved, given, own, other, *outs):
    acc2, acc3, mine, theirs = outs
    _, _, c = here()
    turn_rows(solved, mine, theirs)
    top = (lax.axis_index("layer") == 0).astype(F32)
    place_rows(acc2, given.at[1], h)
    place_rows(acc3, given.at[2], h)
    acc3[...] *= top
    for r, weights, first in ((c, own, 1), (1 - c, other, 0)):
        acc2[r] -= products(weights.at[first], solved)
        acc3[r] -= products(weights.at[first + 1], solved)


def later_kernel(solved, own, other, acc, out, mine, theirs):
    _, _, c = here()
    turn_rows(solved, mine, theirs)
    out[c] = acc[c] - products(own.at[4], solved)
    out[1 - c] = acc[1 - c] - products(other.at[3], solved)


def turn_kernel(*refs):
    *parts, mine, theirs = refs
    cols = parts[0].shape[-1]
    for index in range(0, len(parts), 2):
        level, h = divmod(index // 2, CHUNKS)
        columns = slice(h * cols, (h + 1) * cols)
        mine[level, :, :, columns] = parts[index][...]
        theirs[level, :, :, columns] = parts[index + 1][...]


def last_kernel(*refs):
    *parts, mine, theirs = refs
    a, _, c = here()
    rows, cols = parts[0].shape
    part = mine.shape[2]
    for index, piece in enumerate(parts):
        h, group = divmod(index, 2)
        columns = slice(h * cols, (h + 1) * cols)
        for out, place in ((mine, crossed(a)), (theirs, crossed(a ^ 1))):
            for r in range(2):
                value = piece[at(4 * r + place, part)]
                out[0, (a - c) ^ (2 * group + r), :, columns] = value


def swap_kernel(mine, came, out):
    _, _, c = here()
    cols = came.shape[-1]
    for level in range(out.shape[0]):
        out[level, :, :, at(c, cols)] = mine[level]
        out[level, :, :, at(1 - c, cols)] = came[level]


def output_kernel(first, second, forest, root):
    forest[...] = first[...]
    root[...] = second[...]


def shards(subtree_right_hand, root_rhs, blocks, pattern, forest_inverse, root_inverse):
    layers = lax.axis_size("layer")
    size = blocks.shape[-1]
    part, half = size // 4, size // 2
    width = subtree_right_hand.shape[-1]
    forest = subtree_right_hand.reshape(3, 4, part, width)
    root = root_rhs.reshape(4, part, width)
    blocks = blocks.reshape(6, 4, 4, size, size)
    pattern = pattern.reshape(6, 4, 4)
    inverses = forest_inverse.reshape(3, size, size)
    last_inverse = root_inverse.reshape(size, size)
    both = ("prow", "pcol")
    turn = [(i * 4 + j, j * 4 + i) for i in range(4) for j in range(4)]
    back = [
        [(i * 4 + j, j * 4 + crossed(i ^ k)) for i in range(4) for j in range(4)]
        for k in range(2)
    ]
    hbm = pl.BlockSpec(memory_space=pltpu.HBM)
    dma = pltpu.SemaphoreType.DMA
    run = functools.partial

    def after(*values):
        return lax.optimization_barrier(values)

    def swap(value, axis, k):
        return lax.ppermute(value, axis, [(i, i ^ k) for i in range(4)])

    tokens = []

    def step(how, kernel, outs, *args, in_specs=None, **options):
        count = len(args)
        specs = whole(count) if in_specs is None else list(in_specs)
        chained = bool(tokens)

        def body(*refs):
            ins, refs = refs[:count], refs[count + chained :]
            made, token, held = refs[: len(outs)], refs[len(outs)], refs[len(outs) + 1 :]
            token[...] = jnp.zeros_like(token)
            kernel(*ins, *made, *held)

        *results, token = how(
            body,
            [*outs, ((8, 128), F32)],
            *args,
            *tokens,
            in_specs=specs + whole(chained),
            **options,
        )
        tokens[:] = [token]
        return results

    rows = 2 * size
    wide = width // 2
    cols = wide // CHUNKS
    every = range(CHUNKS)
    block, kept = ((rows, cols), BF16), ((rows, cols), F32)
    sums = ((2, 4, size, cols), F32)
    tall = ((4 * size, cols), BF16)
    turned = ((4, part, cols), BF16)

    side, own, near, far = call(
        pack_kernel,
        [
            ((2, 4, part, wide), BF16),
            ((4 * half + 3 * part, width), BF16),
            ((4 * half + 3 * part, width), BF16),
            ((half + 6 * part, width), BF16),
        ],
        forest,
        root,
        inverses,
        last_inverse,
        in_specs=[hbm] * 4,
        time=2,
        scratch=[
            VMEM((3, 4, part, width), BF16),
            VMEM((4, part, width), BF16),
            VMEM((3, size, size), F32),
            VMEM((size, size), F32),
            dma((4,)),
        ],
        limit=LARGE,
    )
    side = lax.ppermute(side, both, turn)
    far = swap(far, "prow", 2)
    near = swap(near, "prow", 1)
    blocks_other, pattern_other = swap(blocks, "prow", 1), swap(pattern, "prow", 1)
    smem = pl.BlockSpec(memory_space=pltpu.SMEM)

    def masked(first, count, flip):
        (out,) = step(
            call,
            run(mask_kernel, first, flip),
            [((count, 4, size, 4 * size), BF16)],
            pattern_other if flip else pattern,
            blocks_other if flip else blocks,
            in_specs=[smem, hbm],
            scratch=[VMEM((count, 4, 4, size, size), BF16), dma((count,))],
            time=0.3 * count,
        )
        return out

    weights = masked(0, 6, 0)
    side, far, weights = after(side, far, weights)
    fourth = swap(far, "prow", 1)

    def send(outs):
        return swap(outs[2], "pcol", 1)

    def add(outs, came):
        (passed,) = step(call, add_kernel, [block], outs[1], came)
        return outs[0], came, swap(passed, "pcol", 2)

    def solve(level, *terms):
        (answer,) = step(
            call,
            run(solve_kernel, level),
            [block],
            *terms,
            own,
            near,
            scratch=[VMEM(*kept)],
            time=0.3,
        )
        return answer, swap(answer, "prow", 2)

    def join(mine, theirs):
        shape = (mine.shape[0], 4, part, width)
        return step(call, swap_kernel, [(shape, BF16)], mine, theirs)[0]

    message = ((2 * rows, cols), BF16)
    cross = swap(side, "prow", 2)
    sides = (side, swap(side, "prow", 1), cross, swap(cross, "prow", 1))
    first_other = masked(0, 1, 1)
    solved, outs, came, terms, pieces, acc2, acc3 = ({} for _ in range(7))
    turns = [{}, {}, {}]

    def early(h):
        acc2[h], acc3[h], *turns[0][h] = step(
            call,
            run(early_kernel, h),
            [sums, sums, turned, turned],
            solved[h],
            given,
            weights,
            others,
            time=0.7,
        )

    def later(h):
        acc3[h], *turns[1][h] = step(
            call,
            later_kernel,
            [sums, turned, turned],
            solved[h],
            weights,
            others,
            acc3[h],
            time=0.4,
        )

    def middle(h, pair, acc):
        solved[h], *outs[h] = step(
            call,
            run(middle_kernel, pair, pair - 1),
            [tall, kept, kept, message],
            *pieces[h],
            weights,
            others,
            acc[h],
            time=0.4,
        )
        came[h] = send(outs[h])

    *values, given, o0, o2, first_message = step(
        call,
        first_kernel,
        [tall] * CHUNKS + [((3, 2, 4, part, wide), BF16), kept, kept, message],
        *sides,
        own,
        near,
        far,
        fourth,
        weights,
        first_other,
        scratch=[VMEM((4, size, wide), BF16), VMEM((2, 4, size, cols), F32)],
        time=1.5,
    )
    for h in every:
        solved[h] = values[h]
        if h > 0:
            o0, o2, first_message = step(
                call,
                run(second_kernel, h),
                [kept, kept, message],
                solved[h],
                given,
                weights,
                first_other,
                scratch=[VMEM((2, 4, size, cols), F32)],
                time=0.4,
            )
        outs[h] = o0, o2, first_message
        came[h] = send(outs[h])
    for h in every:
        terms[h] = add(outs[h], came[h])
        if h == 0:
            others = masked(1, 5, 1)
    for h in every:
        early(h)
    for h in every:
        pieces[h] = solve(1, *terms[h])
    for h in every:
        middle(h, 3, acc2)
    for h in every:
        terms[h] = add(outs[h], came[h])
    for h in every:
        later(h)
    for h in every:
        pieces[h] = solve(2, *terms[h])
    for h in every:
        middle(h, 5, acc3)
    for h in every:
        turns[2][h] = step(call, rows_kernel, [turned, turned], solved[h])
    parts = [value for level in turns for h in every for value in level[h]]
    mine, theirs = step(call, turn_kernel, [((3, 4, part, wide), BF16)] * 2, *parts)
    theirs = swap(theirs, "prow", 1)
    for h in every:
        terms[h] = add(outs[h], came[h])
        if h == 0:
            pass
    for h in every:
        if h == 1:
            forest_rows = join(mine, theirs)
        (total,) = step(call, sum_kernel, [block if layers == 2 else kept], *terms[h])
        if layers == 2:
            terms[h] = total, lax.ppermute(total, "layer", [(0, 1), (1, 0)])
        else:
            terms[h] = (lax.psum(total, "layer"),)
    forest_out = lax.ppermute(forest_rows, both, back[0])
    for h in every:
        pieces[h] = solve(3, *terms[h])
    lasts = [piece for h in every for piece in pieces[h]]
    mine, theirs = step(call, last_kernel, [((1, 4, part, wide), BF16)] * 2, *lasts)
    root_rows = join(mine, swap(theirs, "prow", 1))
    root_out = lax.ppermute(root_rows, both, back[0])
    forest_out, root_out = step(
        call,
        output_kernel,
        [((3, 4, part, width), BF16), ((1, 4, part, width), BF16)],
        forest_out,
        root_out,
    )
    return forest_out.reshape(1, 3 * size, width), root_out.reshape(size, width)


def solution(mesh):
    placed = (
        P("layer", ("prow", "pcol"), None),
        P(("prow", "pcol"), None),
        P("layer", None, "prow", "pcol", None, None, None, None),
        P("layer", None, "prow", "pcol", None, None),
        P("layer", None, "prow", "pcol", None, None),
        P("prow", "pcol", None, None),
    )
    return jax.shard_map(
        shards,
        mesh=mesh,
        in_specs=placed,
        out_specs=(P("layer", ("prow", "pcol"), None), P(("prow", "pcol"), None)),
        check_vma=False,
    )
```

```python
import functools

import jax
import jax.numpy as jnp
from jax import lax
from jax.experimental import pallas as pl
from jax.experimental.pallas import tpu as pltpu
from jax.sharding import PartitionSpec as P

F32 = jnp.float32
BF16 = jnp.bfloat16
VMEM = pltpu.VMEM
MIB = 1024 * 1024
LARGE = 60
CHUNKS = 2


def whole(count):
    return [pl.BlockSpec(memory_space=VMEM)] * count


def cost(micros):
    return pl.CostEstimate(
        flops=0, bytes_accessed=int(micros * 3.69e6), transcendentals=0
    )


def call(kernel, outs, *args, scratch=(), in_specs=None, limit=32, time=0.1):
    return pl.pallas_call(
        kernel,
        out_shape=[jax.ShapeDtypeStruct(shape, dtype) for shape, dtype in outs],
        in_specs=whole(len(args)) if in_specs is None else in_specs,
        out_specs=whole(len(outs)),
        scratch_shapes=list(scratch),
        compiler_params=pltpu.CompilerParams(vmem_limit_bytes=limit * MIB),
        cost_estimate=cost(time),
    )(*args)


def dot(left, right):
    return jnp.dot(left, right, preferred_element_type=F32)


def split(value):
    high = value.astype(BF16)
    return high, (value - high.astype(F32)).astype(BF16)


def precise(inverse, value):
    ih, il = inverse
    vh, vl = split(value)
    return dot(
        jnp.concatenate([ih, ih, il], axis=1), jnp.concatenate([vh, vl, vh], axis=0)
    )


def packed(inverse):
    high, low = split(inverse)
    half = high.shape[0] // 2
    return jnp.concatenate([high[:half], high[half:], low[:half], low[half:]], axis=1)


def unpacked(value):
    size = value.shape[1] // 4
    parts = [value[:, i * size : (i + 1) * size] for i in range(4)]
    return (
        jnp.concatenate(parts[:2], axis=0),
        jnp.concatenate(parts[2:], axis=0),
    )


def here():
    a, b = lax.axis_index("prow"), lax.axis_index("pcol")
    return a, b, a % 2


def at(start, length):
    return pl.ds(pl.multiple_of(start * length, length), length)


def crossed(index):
    return (4 - index) % 4


def pack_kernel(forest, root, inverses, last, side, own, near, far, *rest):
    held, top, inverse, final, sems = rest
    a, b, _ = here()
    part, wide = held.shape[2], side.shape[-1]
    half = final.shape[0] // 2
    moves = [
        pltpu.make_async_copy(source, out, sems.at[i])
        for i, (source, out) in enumerate(
            (
                (forest, held),
                (inverses, inverse),
                (root, top),
                (last, final),
            )
        )
    ]
    for move in moves:
        move.start()

    def piece(rows, k):
        there = a ^ k
        base, columns = there - there % 2, at(there % 2, wide)
        return jnp.concatenate(
            [rows[base, :, columns], rows[base + 1, :, columns]], axis=1
        )

    moves[0].wait()
    for i in range(2):
        side[i] = held[0, :, :, at((b % 2) ^ i, wide)]
    for i in range(1, 4):
        moves[i].wait()
    for out, slots in ((own, (0,)), (near, (1,)), (far, (2, 3))):
        out[:half] = packed(inverse[0])
        start = half
        for k in slots:
            for rows in (held.at[1], held.at[2], top):
                out[start : start + part] = piece(rows, k)
                start += part
    for value in (inverse[1], inverse[2], final[...]):
        for out in (own, near):
            out[start - 3 * part : start - 3 * part + half] = packed(value)
        start += half


def masked_rows(n, pattern, block, out, index):
    b, base = lax.axis_index("pcol"), index - index % 2
    size = block.shape[-1]
    for j in range(4):
        for k in range(4):
            value = block[b ^ j, base ^ k]
            out[j, :, k * size : (k + 1) * size] = jnp.where(
                pattern[n, b ^ j, base ^ k] != 0, value, jnp.zeros_like(value)
            )


def mask_kernel(first, flip, pattern, blocks, out, held, sems):
    a, _, _ = here()
    moves = [
        pltpu.make_async_copy(blocks.at[first + n], held.at[n], sems.at[n])
        for n in range(out.shape[0])
    ]
    for move in moves:
        move.start()
    for n, move in enumerate(moves):
        move.wait()
        masked_rows(first + n, pattern, held.at[n], out.at[n], a ^ flip)


def products(weights, solved):
    four, size, depth = weights.shape
    value = dot(weights[...].reshape(four * size, depth), solved[...])
    return value.reshape(four, size, solved.shape[1])


def send_sums(acc, own, other, solved, o0, o2, message):
    _, _, c = here()
    rows, size = o0.shape[0], own.shape[1]
    for weights, r in ((own, c), (other, 1 - c)):
        value = acc[r] - products(weights, solved)
        o0[at(r, size)] = value[0]
        o2[at(r, size)] = value[2]
        message[at(r, size)] = value[3].astype(message.dtype)
        message[at(2 + r, size)] = value[1].astype(message.dtype)


def place_rows(acc, given, h):
    _, b, _ = here()
    part, cols = given.shape[2], acc.shape[-1]
    acc[...] = jnp.zeros_like(acc)
    value = given[:, :, :, h * cols : (h + 1) * cols]
    acc[:, :, at(b, part)] = value.astype(F32)


def first_kernel(g0, g1, g2, g3, m0, m1, m2, m3, own, other, *rest):
    *solved, given, o0, o2, message, rows, acc = rest
    a, b, c = here()
    part, cols = g0.shape[-2], o0.shape[-1]
    size = 4 * part
    half = size // 2
    for m, piece in enumerate((g0, g1, g2, g3)):
        for u in range(4):
            rows[u, at(a ^ m, part)] = piece[m % 2, u]
    for m, packet in enumerate((m0, m1, m2, m3)):
        high, low = unpacked(packet[:half])
        right = rows[a ^ m]
        answer = dot(
            jnp.concatenate([high, low], axis=1),
            jnp.concatenate([right, right], axis=0),
        ).astype(BF16)
        for h, out in enumerate(solved):
            out[at(m ^ c, size)] = answer[:, h * cols : (h + 1) * cols]
        start = half + (3 * part if m == 3 else 0)
        wide = given.shape[-1]
        for level in range(3):
            for r in range(2):
                value = packet[start : start + part, r * wide : (r + 1) * wide]
                given[level, r, a ^ b ^ m] = value
            start += part
    place_rows(acc, given.at[0], 0)
    send_sums(acc, own.at[0], other.at[0], solved[0], o0, o2, message)


def second_kernel(h, solved, given, own, other, o0, o2, message, acc):
    place_rows(acc, given.at[0], h)
    send_sums(acc, own.at[0], other.at[0], solved, o0, o2, message)


def add_kernel(kept, came, out):
    out[...] = (kept[...] + came[: kept.shape[0]].astype(F32)).astype(out.dtype)


def summed(terms):
    rows = terms[-1].shape[0]
    total = terms[0][...].astype(F32)
    for term in terms[1:]:
        total += term[term.shape[0] - rows :].astype(F32)
    return total


def sum_kernel(*refs):
    refs[-1][...] = summed(refs[:-1]).astype(refs[-1].dtype)


def solve_kernel(level, *refs):
    *terms, own, near, out, value = refs
    _, _, c = here()
    value[...] = summed(terms)
    size = value.shape[0] // 2
    half = size // 2
    start = near.shape[0] - (4 - level) * half
    for message, r in ((own, c), (near, 1 - c)):
        inverse = unpacked(message[start : start + half])
        out[at(r, size)] = precise(inverse, value[at(r, size)]).astype(out.dtype)


def middle_kernel(own_at, other_at, s, far, own, other, acc, solved, *outs):
    rows = s.shape[0]
    solved[:rows] = s[...]
    solved[rows:] = far[...]
    send_sums(acc, own.at[own_at], other.at[other_at], solved, *outs)


def turn_rows(solved, mine, theirs):
    a, _, c = here()
    part = mine.shape[1]
    for out, index in ((mine, crossed(a)), (theirs, crossed(a ^ 1))):
        for k in range(4):
            out[(a - c) ^ k] = solved[at(4 * k + index, part)]


def rows_kernel(solved, mine, theirs):
    turn_rows(solved, mine, theirs)


def early_kernel(h, solved, given, own, other, *outs):
    acc2, acc3, mine, theirs = outs
    _, _, c = here()
    turn_rows(solved, mine, theirs)
    top = (lax.axis_index("layer") == 0).astype(F32)
    place_rows(acc2, given.at[1], h)
    place_rows(acc3, given.at[2], h)
    acc3[...] *= top
    for r, weights, first in ((c, own, 1), (1 - c, other, 0)):
        acc2[r] -= products(weights.at[first], solved)
        acc3[r] -= products(weights.at[first + 1], solved)


def later_kernel(solved, own, other, acc, out, mine, theirs):
    _, _, c = here()
    turn_rows(solved, mine, theirs)
    out[c] = acc[c] - products(own.at[4], solved)
    out[1 - c] = acc[1 - c] - products(other.at[3], solved)


def turn_kernel(*refs):
    *parts, mine, theirs = refs
    cols = parts[0].shape[-1]
    for index in range(0, len(parts), 2):
        level, h = divmod(index // 2, CHUNKS)
        columns = slice(h * cols, (h + 1) * cols)
        mine[level, :, :, columns] = parts[index][...]
        theirs[level, :, :, columns] = parts[index + 1][...]


def last_kernel(*refs):
    *parts, mine, theirs = refs
    a, _, c = here()
    rows, cols = parts[0].shape
    part = mine.shape[2]
    for index, piece in enumerate(parts):
        h, group = divmod(index, 2)
        columns = slice(h * cols, (h + 1) * cols)
        for out, place in ((mine, crossed(a)), (theirs, crossed(a ^ 1))):
            for r in range(2):
                value = piece[at(4 * r + place, part)]
                out[0, (a - c) ^ (2 * group + r), :, columns] = value


def swap_kernel(mine, came, out):
    _, _, c = here()
    cols = came.shape[-1]
    for level in range(out.shape[0]):
        out[level, :, :, at(c, cols)] = mine[level]
        out[level, :, :, at(1 - c, cols)] = came[level]


def output_kernel(first, second, forest, root):
    forest[...] = first[...]
    root[...] = second[...]


def shards(subtree_right_hand, root_rhs, blocks, pattern, forest_inverse, root_inverse):
    layers = lax.axis_size("layer")
    size = blocks.shape[-1]
    part, half = size // 4, size // 2
    width = subtree_right_hand.shape[-1]
    forest = subtree_right_hand.reshape(3, 4, part, width)
    root = root_rhs.reshape(4, part, width)
    blocks = blocks.reshape(6, 4, 4, size, size)
    pattern = pattern.reshape(6, 4, 4)
    inverses = forest_inverse.reshape(3, size, size)
    last_inverse = root_inverse.reshape(size, size)
    both = ("prow", "pcol")
    turn = [(i * 4 + j, j * 4 + i) for i in range(4) for j in range(4)]
    back = [
        [(i * 4 + j, j * 4 + crossed(i ^ k)) for i in range(4) for j in range(4)]
        for k in range(2)
    ]
    hbm = pl.BlockSpec(memory_space=pltpu.HBM)
    dma = pltpu.SemaphoreType.DMA
    run = functools.partial

    def after(*values):
        return lax.optimization_barrier(values)

    def swap(value, axis, k):
        return lax.ppermute(value, axis, [(i, i ^ k) for i in range(4)])

    tokens = []

    def step(how, kernel, outs, *args, in_specs=None, **options):
        count = len(args)
        specs = whole(count) if in_specs is None else list(in_specs)
        chained = bool(tokens)

        def body(*refs):
            ins, refs = refs[:count], refs[count + chained :]
            made, token, held = refs[: len(outs)], refs[len(outs)], refs[len(outs) + 1 :]
            token[...] = jnp.zeros_like(token)
            kernel(*ins, *made, *held)

        *results, token = how(
            body,
            [*outs, ((8, 128), F32)],
            *args,
            *tokens,
            in_specs=specs + whole(chained),
            **options,
        )
        tokens[:] = [token]
        return results

    rows = 2 * size
    wide = width // 2
    cols = wide // CHUNKS
    every = range(CHUNKS)
    block, kept = ((rows, cols), BF16), ((rows, cols), F32)
    sums = ((2, 4, size, cols), F32)
    tall = ((4 * size, cols), BF16)
    turned = ((4, part, cols), BF16)

    side, own, near, far = call(
        pack_kernel,
        [
            ((2, 4, part, wide), BF16),
            ((4 * half + 3 * part, width), BF16),
            ((4 * half + 3 * part, width), BF16),
            ((half + 6 * part, width), BF16),
        ],
        forest,
        root,
        inverses,
        last_inverse,
        in_specs=[hbm] * 4,
        time=2,
        scratch=[
            VMEM((3, 4, part, width), BF16),
            VMEM((4, part, width), BF16),
            VMEM((3, size, size), F32),
            VMEM((size, size), F32),
            dma((4,)),
        ],
        limit=LARGE,
    )
    side = lax.ppermute(side, both, turn)
    far = swap(far, "prow", 2)
    near = swap(near, "prow", 1)
    blocks_other, pattern_other = swap(blocks, "prow", 1), swap(pattern, "prow", 1)
    smem = pl.BlockSpec(memory_space=pltpu.SMEM)

    def masked(first, count, flip):
        (out,) = step(
            call,
            run(mask_kernel, first, flip),
            [((count, 4, size, 4 * size), BF16)],
            pattern_other if flip else pattern,
            blocks_other if flip else blocks,
            in_specs=[smem, hbm],
            scratch=[VMEM((count, 4, 4, size, size), BF16), dma((count,))],
            time=0.3 * count,
        )
        return out

    weights = masked(0, 6, 0)
    side, far, weights = after(side, far, weights)
    fourth = swap(far, "prow", 1)

    def send(outs):
        return swap(outs[2], "pcol", 1)

    def add(outs, came):
        (passed,) = step(call, add_kernel, [block], outs[1], came)
        return outs[0], came, swap(passed, "pcol", 2)

    def solve(level, *terms):
        (answer,) = step(
            call,
            run(solve_kernel, level),
            [block],
            *terms,
            own,
            near,
            scratch=[VMEM(*kept)],
            time=0.3,
        )
        return answer, swap(answer, "prow", 2)

    def join(mine, theirs):
        shape = (mine.shape[0], 4, part, width)
        return step(call, swap_kernel, [(shape, BF16)], mine, theirs)[0]

    message = ((2 * rows, cols), BF16)
    cross = swap(side, "prow", 2)
    sides = (side, swap(side, "prow", 1), cross, swap(cross, "prow", 1))
    first_other = masked(0, 1, 1)
    solved, outs, came, terms, pieces, acc2, acc3 = ({} for _ in range(7))
    turns = [{}, {}, {}]

    def early(h):
        acc2[h], acc3[h], *turns[0][h] = step(
            call,
            run(early_kernel, h),
            [sums, sums, turned, turned],
            solved[h],
            given,
            weights,
            others,
            time=0.7,
        )

    def later(h):
        acc3[h], *turns[1][h] = step(
            call,
            later_kernel,
            [sums, turned, turned],
            solved[h],
            weights,
            others,
            acc3[h],
            time=0.4,
        )

    def middle(h, pair, acc):
        solved[h], *outs[h] = step(
            call,
            run(middle_kernel, pair, pair - 1),
            [tall, kept, kept, message],
            *pieces[h],
            weights,
            others,
            acc[h],
            time=0.4,
        )
        came[h] = send(outs[h])

    *values, given, o0, o2, first_message = step(
        call,
        first_kernel,
        [tall] * CHUNKS + [((3, 2, 4, part, wide), BF16), kept, kept, message],
        *sides,
        own,
        near,
        far,
        fourth,
        weights,
        first_other,
        scratch=[VMEM((4, size, wide), BF16), VMEM((2, 4, size, cols), F32)],
        time=1.5,
    )
    for h in every:
        solved[h] = values[h]
        if h > 0:
            o0, o2, first_message = step(
                call,
                run(second_kernel, h),
                [kept, kept, message],
                solved[h],
                given,
                weights,
                first_other,
                scratch=[VMEM((2, 4, size, cols), F32)],
                time=0.4,
            )
        outs[h] = o0, o2, first_message
        came[h] = send(outs[h])
    for h in every:
        terms[h] = add(outs[h], came[h])
        if h == 0:
            others = masked(1, 5, 1)
    for h in every:
        early(h)
    for h in every:
        pieces[h] = solve(1, *terms[h])
    for h in every:
        middle(h, 3, acc2)
    for h in every:
        terms[h] = add(outs[h], came[h])
        later(h)
    for h in every:
        pieces[h] = solve(2, *terms[h])
    for h in every:
        middle(h, 5, acc3)
    for h in every:
        turns[2][h] = step(call, rows_kernel, [turned, turned], solved[h])
    parts = [value for level in turns for h in every for value in level[h]]
    mine, theirs = step(call, turn_kernel, [((3, 4, part, wide), BF16)] * 2, *parts)
    theirs = swap(theirs, "prow", 1)
    for h in every:
        terms[h] = add(outs[h], came[h])
        if h == 0:
            pass
    for h in every:
        if h == 1:
            forest_rows = join(mine, theirs)
        (total,) = step(call, sum_kernel, [block if layers == 2 else kept], *terms[h])
        if layers == 2:
            terms[h] = total, lax.ppermute(total, "layer", [(0, 1), (1, 0)])
        else:
            terms[h] = (lax.psum(total, "layer"),)
    forest_out = lax.ppermute(forest_rows, both, back[0])
    for h in every:
        pieces[h] = solve(3, *terms[h])
    lasts = [piece for h in every for piece in pieces[h]]
    mine, theirs = step(call, last_kernel, [((1, 4, part, wide), BF16)] * 2, *lasts)
    root_rows = join(mine, swap(theirs, "prow", 1))
    root_out = lax.ppermute(root_rows, both, back[0])
    forest_out, root_out = step(
        call,
        output_kernel,
        [((3, 4, part, width), BF16), ((1, 4, part, width), BF16)],
        forest_out,
        root_out,
    )
    return forest_out.reshape(1, 3 * size, width), root_out.reshape(size, width)


def solution(mesh):
    placed = (
        P("layer", ("prow", "pcol"), None),
        P(("prow", "pcol"), None),
        P("layer", None, "prow", "pcol", None, None, None, None),
        P("layer", None, "prow", "pcol", None, None),
        P("layer", None, "prow", "pcol", None, None),
        P("prow", "pcol", None, None),
    )
    return jax.shard_map(
        shards,
        mesh=mesh,
        in_specs=placed,
        out_specs=(P("layer", ("prow", "pcol"), None), P(("prow", "pcol"), None)),
        check_vma=False,
    )
```
